128 devices in a mesh: band: 16 (over y, x), obs: 8 (over z, core).
Axes of the slice: x: 4, y: 4, z: 4, core: 2. Of those that a mesh axis runs over, the one named last changes fastest.
Arguments:
- obs_values: bfloat16 [24, 262144], P(None, ('band', 'obs')), may hold values from -6 to 6
- obs_tile: int32 [262144], P(('band', 'obs')), may hold values from 0 to 255, as said below
- obs_row: int32 [262144], P(('band', 'obs')), may hold values from 0 to 31
- obs_col: int32 [262144], P(('band', 'obs')), may hold values from 0 to 89
- obs_frac: float32 [2, 262144], P(None, ('band', 'obs')), may hold values from 0 to 1
- tile_place: int32 [256], replicated, may hold values from 0 to 255, as said below
- length_scale: float32 [2], replicated, may hold values from 0.8 to 1.4
- conv_weight: bfloat16 [5, 5, 25, 256], replicated, may hold values from -0.25 to 0.25
- conv_bias: float32 [256], replicated, may hold values from -1.5 to 1.5
Outputs:
- encoded: bfloat16 [256, 720, 256], P(('band', 'obs'))
The draws below stay inside these ranges and needn't reach their ends.
Inputs may be any that keep to these rules, and one draw needn't show every extreme that they name: `obs_tile`: the owner of tile t is t mod 16. Among the 2048 observations of one device, at most 512 lie in tiles of one owner; one owner, the same for all devices, has exactly 512 from every device. tile_place is a permutation; the tiles d + 16 k of one owner d lie in 16 different latitude bands.
All inputs are finite; a program needn't handle non-finite values.
Results may differ from the reference program's by a relative error of at most 0.0057.
Values may be sent and summed in bfloat16 or wider, within the bound.
No kernel may reach another device: no remote copies, remote signals or barrier semaphores. Data moves between devices by JAX's collectives and lax.ppermute only.
A program may use at most 128 MiB of HBM per device.

```python
import math
import jax
import jax.numpy as jnp
from jax import lax

CH = 24
LON = 1440
FEAT = 256
OBS_DEV = 2048
CAP = 512
C1 = 25
LAT_DEV = 32
LAT = 512
TQ = 90
NTILE = 256
OBS = 262144
N_BAND = 16


def draw_tile_place(key, part):
    key = jax.random.fold_in(key, 11)
    key_shift, key_block, key_offset = jax.random.split(key, 3)
    band_shift = jax.random.permutation(key_shift, N_BAND)
    block_shift = jax.random.permutation(key_block, N_BAND)
    band_offset = jax.random.randint(key_offset, (N_BAND,), 0, N_BAND)
    slot_index = jnp.arange(N_BAND)[:, None]
    owner_index = jnp.arange(N_BAND)[None, :]
    band_of = (band_shift[slot_index] + owner_index) % N_BAND
    block_of = (block_shift[slot_index] + band_offset[band_of]) % N_BAND
    return (band_of * N_BAND + block_of).reshape(-1).astype(jnp.int32)


def tile_numbers(key):
    key = jax.random.fold_in(key, 23)
    key_hot, key_blocks = jax.random.split(key)
    hot_owner = jax.random.randint(key_hot, (), 0, N_BAND)
    device_count = OBS // OBS_DEV
    block_keys = jax.random.split(key_blocks, device_count)

    def one_block(block_key):
        key_slots, key_order, key_within = jax.random.split(block_key, 3)
        others = jax.random.permutation(key_slots, (N_BAND - 1) * CAP)[:OBS_DEV - CAP] // CAP
        others = others + (others >= hot_owner).astype(jnp.int32)
        owners = jnp.concatenate([jnp.zeros((CAP,), jnp.int32) + hot_owner, others.astype(jnp.int32)])
        owners = jax.random.permutation(key_order, owners)
        within = jax.random.randint(key_within, (OBS_DEV,), 0, N_BAND)
        return owners + N_BAND * within
    return jax.vmap(one_block)(block_keys).reshape(-1).astype(jnp.int32)


def cluster_plan(key):
    key = jax.random.fold_in(key, 31)
    key_row, key_col, key_join = jax.random.split(key, 3)
    center_row = jax.random.randint(key_row, (NTILE,), 0, LAT_DEV)
    center_col = jax.random.randint(key_col, (NTILE,), 0, TQ)
    joined = jax.random.randint(key_join, (OBS,), 0, 2)
    return (center_row, center_col, joined)


def draw_obs_tile(key, part):
    return tile_numbers(key)


def draw_obs_row(key, part):
    tiles = tile_numbers(key)
    center_row, center_col, joined = cluster_plan(key)
    key = jax.random.fold_in(key, 41)
    spread = jax.random.randint(key, (OBS,), 0, LAT_DEV)
    return jnp.where(joined == 1, center_row[tiles], spread).astype(jnp.int32)


def draw_obs_col(key, part):
    tiles = tile_numbers(key)
    center_row, center_col, joined = cluster_plan(key)
    key = jax.random.fold_in(key, 43)
    spread = jax.random.randint(key, (OBS,), 0, TQ)
    return jnp.where(joined == 1, center_col[tiles], spread).astype(jnp.int32)


def shard_levels(stream_key, extent, shards, least, high):
    def one(dim, shards_of):
        steps = jax.random.uniform(jax.random.fold_in(jax.random.fold_in(stream_key, 6), dim), (shards_of,), jnp.float32, least / len(shards), high / len(shards))
        return jnp.repeat(jnp.exp(steps), extent[dim] // shards_of).reshape((-1,) + (1,) * (len(extent) - dim - 1))

    loudness = one(*shards[0])
    for cut in shards[1:]:
        loudness = loudness * one(*cut)
    return loudness


def normal_values(own_key, extent, width, limit, cuts=(), held_as=jnp.bfloat16):
    loudness = shard_levels(own_key, extent, cuts, -0.22, 0.18) if cuts else 1.0
    result = jax.random.normal(own_key, extent, jnp.float32) * width * loudness
    return jnp.minimum(jnp.maximum(result, -limit), limit).astype(held_as)


def setup_inputs(seed: int = 0) -> dict:
    key_list = jax.random.split(jax.random.key(seed), 10)
    obs_values = normal_values(key_list[0], (CH, OBS), 1.0, 6.0, ((1, 128),))
    obs_tile = draw_obs_tile(jax.random.fold_in(key_list[9], 71), 0)
    obs_row = draw_obs_row(jax.random.fold_in(key_list[9], 71), 0)
    obs_col = draw_obs_col(jax.random.fold_in(key_list[9], 71), 0)
    obs_frac = jnp.clip(1.0 * jax.random.uniform(key_list[4], (2, OBS), jnp.float32) ** shard_levels(key_list[4], (2, OBS), ((1, 128),), -0.2, 0.2), 0.0, 1.0)
    tile_place = draw_tile_place(jax.random.fold_in(key_list[9], 71), 0)
    length_scale = jnp.clip(jnp.exp(jax.random.uniform(key_list[6], (2,), jnp.float32, math.log(0.8), math.log(1.4))), 0.8, 1.4)
    conv_weight = normal_values(key_list[7], (5, 5, C1, FEAT), (25 * C1) ** -0.5, 0.25)
    conv_bias = normal_values(key_list[8], (FEAT,), 0.25, 1.5, (), jnp.float32)
    return {"obs_values": obs_values, "obs_tile": obs_tile, "obs_row": obs_row, "obs_col": obs_col, "obs_frac": obs_frac, "tile_place": tile_place, "length_scale": length_scale, "conv_weight": conv_weight, "conv_bias": conv_bias}


def reference(obs_values, obs_tile, obs_row, obs_col, obs_frac, tile_place, length_scale, conv_weight, conv_bias):
    place_of = tile_place[obs_tile]
    lat_pos = obs_row.astype(jnp.float32) + obs_frac[0]
    lon_pos = obs_col.astype(jnp.float32) + obs_frac[1]
    inv_lat = 0.5 / (length_scale[0] * length_scale[0])
    inv_lon = 0.5 / (length_scale[1] * length_scale[1])
    lat_diff = (jnp.arange(LAT_DEV, dtype=jnp.float32) + 0.5)[None, :] - lat_pos[:, None]
    lon_diff = (jnp.arange(TQ, dtype=jnp.float32) + 0.5)[None, :] - lon_pos[:, None]
    lat_weight = jnp.exp(-(lat_diff * lat_diff) * inv_lat)
    lon_weight = jnp.exp(-(lon_diff * lon_diff) * inv_lon).astype(jnp.bfloat16)
    extended = jnp.concatenate([obs_values.astype(jnp.float32).T, jnp.ones((OBS, 1), jnp.float32)], axis=1)
    left_factor = (extended[:, :, None] * lat_weight[:, None, :]).astype(jnp.bfloat16).reshape(OBS, C1 * LAT_DEV)
    block_count = OBS // 512
    left_blocks = left_factor.reshape(block_count, 512, C1 * LAT_DEV)
    right_blocks = lon_weight.reshape(block_count, 512, TQ)
    place_blocks = place_of.reshape(block_count, 512)

    def add_block(running, pieces):
        left_part, right_part, where = pieces
        outer = left_part.astype(jnp.float32)[:, :, None] * right_part.astype(jnp.float32)[:, None, :]
        return running + jax.ops.segment_sum(outer, where, num_segments=NTILE), None

    start = jnp.zeros((NTILE, C1 * LAT_DEV, TQ), jnp.float32)
    tile_sums, _ = lax.scan(add_block, start, (left_blocks, right_blocks, place_blocks))
    grid_sums = tile_sums.reshape(N_BAND, N_BAND, C1, LAT_DEV, TQ).transpose(2, 0, 3, 1, 4).reshape(C1, LAT, LON)
    density = grid_sums[CH]
    feature = jnp.concatenate([grid_sums[:CH] / jnp.maximum(density, 1.0)[None], jnp.log(1.0 + density)[None]], axis=0).astype(jnp.bfloat16)
    padded = jnp.pad(feature.astype(jnp.float32), ((0, 0), (2, 1), (0, 0)))
    wrapped = jnp.concatenate([padded[:, :, -2:], padded, padded[:, :, :2]], axis=2)
    conv_out = lax.conv_general_dilated(wrapped[None], conv_weight.astype(jnp.float32), (2, 2), "VALID", dimension_numbers=("NCHW", "HWIO", "NHWC"), precision=lax.Precision.HIGHEST)[0]
    return (conv_out + conv_bias).astype(jnp.bfloat16)
```

```python
import functools

import jax
import jax.numpy as jnp
from jax import lax
from jax.experimental import pallas as pl
from jax.experimental.pallas import tpu as pltpu
from jax.sharding import PartitionSpec as P

LON = 1440
ROWS_DEV = 4
BANDS = 16
TQ = 90
HALF = TQ // 2
HALF_PAD = 48
BOX = 256
EXTRA = 8
ROW_CODE = 24
ROW_LAT = 25
ROW_LON = 28
ROW_NOTE = 31
PAY = 32
F32 = jnp.float32
BF16 = jnp.bfloat16


def dot_nt(left, right):
    return lax.dot_general(left, right, (((1,), (1,)), ((), ())), preferred_element_type=F32)


def iota(shape, dim):
    return lax.broadcasted_iota(jnp.int32, shape, dim)


def ones_where(mask):
    return jnp.where(mask, 1.0, 0.0)


def ranks(member):
    chunks = len(member)
    rows = chunks * BANDS
    stacked = jnp.concatenate(member, axis=0).astype(BF16)
    before = ones_where(iota((BOX, BOX), 0) < iota((BOX, BOX), 1)).astype(BF16)
    at, of = iota((rows, rows), 0), iota((rows, rows), 1)
    earlier = ones_where(((of & 15) == (at & 15)) & ((of >> 4) < (at >> 4))).astype(BF16)
    inside = jnp.dot(stacked, before, preferred_element_type=F32)
    base = jnp.sum(jnp.dot(earlier, stacked, preferred_element_type=F32), axis=1, keepdims=True)
    place = inside + base
    return [
        jnp.sum(member[k] * place[k * BANDS : (k + 1) * BANDS], axis=0, keepdims=True)
        for k in range(chunks)
    ]


def bucket(payload, group, position, left_ref, right_ref, k):
    lanes = slice(k * BOX, (k + 1) * BOX)
    for g in range(left_ref.shape[0] // PAY):
        left_ref[g * PAY : (g + 1) * PAY, lanes] = jnp.where(group == g, payload, 0.0).astype(BF16)
    right_ref[:, lanes] = ones_where(iota((right_ref.shape[0], BOX), 0) == position).astype(BF16)


def split3(value):
    high = value.astype(BF16).astype(F32)
    rest = value - high
    middle = rest.astype(BF16).astype(F32)
    return high, middle, rest - middle


def pack_kernel(values_ref, tile_ref, row_ref, col_ref, frac_ref, place_ref, out_ref, left_ref, right_ref):
    chunks = tile_ref.shape[0] * 128 // BOX

    def wide(ref, k):
        return jnp.concatenate([ref[2 * k : 2 * k + 1, :], ref[2 * k + 1 : 2 * k + 2, :]], axis=1)

    table = jnp.broadcast_to(wide(place_ref, 0).astype(F32), (8, BOX)).astype(BF16)
    ones = jnp.ones((8, BOX), BF16)
    lines = iota((BOX, BOX), 0)
    eight = iota((8, BOX), 0)
    counts = jnp.zeros((8, BOX), F32)
    bands, blocks, member = [], [], []
    for k in range(chunks):
        tile_pick = ones_where(lines == wide(tile_ref, k)).astype(BF16)
        place = jnp.dot(table, tile_pick, preferred_element_type=F32)[0:1].astype(jnp.int32)
        counts = counts + dot_nt(ones, ones_where(lines == place).astype(BF16))
        bands.append(place >> 4)
        blocks.append(place & 15)
        member.append(ones_where(iota((BANDS, BOX), 0) == bands[k]))
    rank = ranks(member)
    for k in range(chunks):
        lanes = slice(k * BOX, (k + 1) * BOX)
        lat = split3(wide(row_ref, k).astype(F32) + frac_ref[0:1, lanes])
        lon = split3(wide(col_ref, k).astype(F32) + frac_ref[1:2, lanes])
        tail = jnp.zeros((8, BOX), F32)
        for at, line in enumerate([blocks[k].astype(F32) + 1.0, *lat, *lon]):
            tail = jnp.where(eight == at, line, tail)
        payload = jnp.concatenate([values_ref[:, lanes].astype(F32), tail], axis=0)
        bucket(payload, bands[k], rank[k].astype(jnp.int32), left_ref, right_ref, k)
    packed = dot_nt(left_ref[...], right_ref[...])
    line_of = iota((PAY, BOX), 0)
    for g in range(BANDS):
        rows = slice(g * PAY, (g + 1) * PAY)
        out_ref[rows, :] = jnp.where(line_of == ROW_NOTE, counts[0:1], packed[rows]).astype(BF16)


def regroup_kernel(in_ref, out_ref, left_ref, right_ref):
    chunks = in_ref.shape[0] // PAY
    codes, member, notes = [], [], []
    line_of = iota((PAY, BOX), 0)
    total = jnp.zeros((BANDS, 1), F32)
    for k in range(chunks):
        tail = in_ref[k * PAY + 16 : (k + 1) * PAY, :].astype(F32)
        codes.append(tail[ROW_CODE - 16 : ROW_CODE - 15].astype(jnp.int32) - 1)
        notes.append(tail[ROW_NOTE - 16 : ROW_NOTE - 15])
        member.append(ones_where(iota((BANDS, BOX), 0) == codes[k]))
        total = total + jnp.sum(member[k], axis=1, keepdims=True)
    rank = ranks(member)

    more = jnp.maximum(jnp.broadcast_to(total, (BANDS, 128)).astype(jnp.int32) - 1, 0) >> 7
    lower = ones_where(iota((BANDS, BANDS), 1) < iota((BANDS, BANDS), 0)).astype(BF16)
    first = jnp.dot(lower, more.astype(F32).astype(BF16), preferred_element_type=F32)
    last = first + more.astype(F32)
    first_wide = jnp.concatenate([first, first], axis=1)

    for k in range(chunks):
        payload = in_ref[k * PAY : (k + 1) * PAY, :].astype(F32)
        payload = jnp.where(line_of == ROW_CODE, 1.0, jnp.where(line_of == ROW_NOTE, 0.0, payload))
        place = rank[k].astype(jnp.int32)
        over = jnp.sum(member[k] * first_wide, axis=0, keepdims=True).astype(jnp.int32)
        group = jnp.where(place < 128, codes[k], BANDS - 1 + over + (place >> 7))
        group = jnp.where(codes[k] < 0, -1, group)
        bucket(payload, group, place & 127, left_ref, right_ref, k)
    moved = dot_nt(left_ref[...], right_ref[...])

    note = jnp.concatenate(notes, axis=0)
    of_band = ones_where((iota((BOX, 128), 0) >> 4) == iota((BOX, 128), 1)).astype(BF16)
    band_sums = jnp.dot(note.astype(BF16), of_band, preferred_element_type=F32)
    tile_sums = jnp.broadcast_to(jnp.sum(note, axis=0, keepdims=True), (8, BOX)).astype(jnp.int32)
    tile_more = (jnp.maximum(tile_sums - 1, 0) >> 7).astype(F32).astype(BF16)
    more_sums = jnp.dot(tile_more, of_band, preferred_element_type=F32)
    band_most = jnp.max(jnp.max(band_sums, axis=1, keepdims=True), axis=0, keepdims=True)
    more_most = jnp.max(jnp.max(more_sums, axis=1, keepdims=True), axis=0, keepdims=True)
    over = jnp.where((band_most > BOX - 1) | (more_most > EXTRA), 1.0, 0.0)

    narrow = iota((PAY, 128), 0)
    out_ref[0:PAY, :] = jnp.where(narrow == ROW_NOTE, over, moved[0:PAY]).astype(BF16)
    out_ref[PAY : BANDS * PAY, :] = moved[PAY : BANDS * PAY].astype(BF16)
    block_code = iota((BANDS, 128), 0).astype(F32) + 1.0
    for e in range(EXTRA):
        rows = slice((BANDS + e) * PAY, (BANDS + e + 1) * PAY)
        code = jnp.where((first <= e) & (last > e), block_code, 0.0)
        code = jnp.sum(code, axis=0, keepdims=True)
        out_ref[rows, :] = jnp.where(narrow == ROW_NOTE, code, moved[rows]).astype(BF16)


def sums_kernel(scale_ref, *refs):
    (
        *block_refs,
        feature_ref,
        lower_ref,
        upper_ref,
        over_ref,
        left_ref,
        right_ref,
        sums_ref,
        wide_ref,
        codes_ref,
        codes_smem,
        sem,
    ) = refs
    first_row = (lax.axis_index("obs") * ROWS_DEV).astype(F32)
    scale = jnp.full((8, 128), 1.0, F32)
    inv_lat = 0.5 / (scale * scale_ref[0] * scale_ref[0])
    inv_lon = 0.5 / (scale * scale_ref[1] * scale_ref[1])
    inv_lat, inv_lon = inv_lat[0:1], inv_lon[0:1]
    row_mid = iota((8, 128), 0).astype(F32) + 0.5 + first_row
    line = iota((2 * HALF_PAD, 128), 0)
    past = (line >= HALF_PAD).astype(jnp.int32)
    col_mid = (2 * (line - HALF_PAD * past) + past).astype(F32) + 0.5
    keep = iota((PAY, 128), 0) <= ROW_CODE
    blocks = len(block_refs)
    tall = 2 * HALF_PAD

    lane = iota((8, 128), 1)
    sub = iota((8, 128), 0)
    codes = jnp.zeros((8, 128), F32)
    for k in range(blocks):
        for e in range(EXTRA):
            at = (BANDS + e) * PAY + 16
            note = block_refs[k][at : at + 16, :].astype(F32)[15:16]
            codes = jnp.where((lane == e) & (sub == k), note, codes)
    codes_ref[...] = codes.astype(jnp.int32)
    copy = pltpu.make_async_copy(codes_ref, codes_smem, sem)
    copy.start()

    def factors(start):
        for k in range(blocks):
            lanes = slice(k * 128, (k + 1) * 128)
            block = block_refs[k][pl.ds(start, PAY), :].astype(F32)
            lat_at = block[ROW_LAT : ROW_LAT + 1] + block[ROW_LAT + 1 : ROW_LAT + 2]
            lat_at = lat_at + block[ROW_LAT + 2 : ROW_LAT + 3]
            lon_at = block[ROW_LON : ROW_LON + 1] + block[ROW_LON + 1 : ROW_LON + 2]
            lon_at = lon_at + block[ROW_LON + 2 : ROW_LON + 3]
            lat_diff = row_mid - lat_at
            lat_weight = jnp.exp(-(lat_diff * lat_diff) * inv_lat)
            lon_diff = col_mid - lon_at
            lon_weight = jnp.exp(-(lon_diff * lon_diff) * inv_lon)
            value = jnp.where(keep, block, 0.0)
            present = block[ROW_CODE : ROW_CODE + 1]
            for r in range(ROWS_DEV):
                weight = lat_weight[r : r + 1]
                left_ref[r * PAY : (r + 1) * PAY, lanes] = (value * weight).astype(BF16)
                left_ref[(ROWS_DEV + r) * PAY : (ROWS_DEV + r + 1) * PAY, lanes] = jnp.broadcast_to(
                    present * weight, (PAY, 128)
                ).astype(BF16)
            right_ref[:, lanes] = lon_weight.astype(BF16)

    def main(p, carry):
        factors(pl.multiple_of(p * PAY, PAY))
        start = pl.multiple_of((p + 1) * tall, tall)
        sums_ref[pl.ds(start, tall), :] = dot_nt(right_ref[...], left_ref[...])
        return carry

    sums_ref[0:tall, :] = jnp.zeros((tall, 256), F32)
    lax.fori_loop(0, BANDS, main, 0)
    copy.wait()
    used = jnp.int32(0)
    for e in range(EXTRA):
        for k in range(blocks):
            used = jnp.where(codes_smem[k, e] > 0, e + 1, used)

    def extra(e, carry):
        factors(pl.multiple_of((BANDS + e) * PAY, PAY))
        for k in range(blocks):
            lanes = slice(k * 128, (k + 1) * 128)
            start = pl.multiple_of(codes_smem[k, e] * tall, tall)
            sums_ref[pl.ds(start, tall), :] += dot_nt(right_ref[:, lanes], left_ref[:, lanes])
        return carry

    lax.fori_loop(0, used, extra, 0)

    channel = iota((HALF_PAD, 128), 1) & (PAY - 1)
    for block in range(BANDS):
        for odd in range(2):
            start = (2 * (block + 1) + odd) * HALF_PAD
            total = sums_ref[start : start + HALF_PAD, 0:128]
            density = sums_ref[start : start + HALF_PAD, 128:256]
            feature = jnp.where(
                channel < 24,
                total / jnp.maximum(density, 1.0),
                jnp.where(channel == 24, jnp.log(1.0 + density), 0.0),
            )
            wide_ref[block * HALF : (block + 1) * HALF, odd * 128 : (odd + 1) * 128] = feature[:HALF]
    feature_ref[...] = wide_ref[...].astype(BF16)
    lower_ref[...] = jnp.concatenate([wide_ref[:, 64:128], wide_ref[:, 192:256]], axis=1).astype(BF16)
    top = jnp.concatenate([wide_ref[0:368, 0:32], wide_ref[0:368, 128:160]], axis=1)
    rest = jnp.concatenate([wide_ref[368:720, 0:32], wide_ref[368:720, 128:160]], axis=1)
    rest = jnp.concatenate([rest, jnp.zeros((16, 64), F32)], axis=0)
    upper_ref[...] = jnp.concatenate([top, rest], axis=1).astype(BF16)
    over = block_refs[0][0:PAY, :].astype(F32)[ROW_NOTE:PAY]
    for k in range(1, blocks):
        over = jnp.maximum(over, block_refs[k][0:PAY, :].astype(F32)[ROW_NOTE:PAY])
    over_ref[...] = jnp.broadcast_to(over, (8, 128))


def conv_kernel(feature_ref, lower_ref, upper_ref, weight_ref, bias_ref, out_ref, wide_ref, w_ref):
    columns = feature_ref.shape[0]
    w_ref[...] = jnp.zeros(w_ref.shape, BF16)
    channels = weight_ref.shape[2]
    zero = jnp.zeros((PAY - channels, 256), BF16)

    def put(shift, at, out_row, tap, odd):
        e = 2 * (shift + 1) + odd
        if e < 5:
            part = jnp.concatenate([weight_ref[tap, e].astype(F32), zero.astype(F32)], axis=0)
            w_ref[shift + 1, at : at + PAY, out_row * 256 : (out_row + 1) * 256] = part.astype(BF16)

    for shift in (-1, 0, 1):
        for odd in range(2):
            for row in range(ROWS_DEV):
                for out_row in range(2):
                    tap = row - 2 * out_row + 2
                    if 0 <= tap < 5:
                        put(shift, odd * 128 + row * PAY, out_row, tap, odd)
            for row in range(2):
                put(shift, 256 + odd * 64 + row * PAY, 0, row, odd)
            put(shift, 384 + odd * 32, 1, 4, odd)

    edge = 8
    wide_ref[edge : edge + columns, 0:256] = feature_ref[...].astype(F32)
    wide_ref[edge : edge + columns, 256:384] = lower_ref[...].astype(F32)
    upper = upper_ref[...].astype(F32)
    wide_ref[edge : edge + 368, 384:448] = upper[:, 0:64]
    wide_ref[edge + 368 : edge + columns, 384:448] = upper[: columns - 368, 64:128]
    wide_ref[edge : edge + columns, 448:512] = jnp.zeros((columns, 64), F32)
    wide_ref[edge - 1 : edge, :] = wide_ref[edge + columns - 1 : edge + columns, :]
    wide_ref[edge + columns : edge + columns + 1, :] = wide_ref[edge : edge + 1, :]

    total = None
    for shift in (-1, 0, 1):
        moved = wide_ref[edge + shift : edge + shift + columns, :].astype(BF16)
        part = jnp.dot(moved, w_ref[shift + 1], preferred_element_type=F32)
        total = part if total is None else total + part
    bias = bias_ref[...]
    out_ref[0] = (total[:, 0:256] + bias).astype(BF16)
    out_ref[1] = (total[:, 256:512] + bias).astype(BF16)


def params(mib):
    return pltpu.CompilerParams(vmem_limit_bytes=mib * 2**20)


def vmem():
    return pl.BlockSpec(memory_space=pltpu.VMEM)


def fast_features(values, tile, row, col, frac, place, scale):
    arrivals = tile.shape[0]
    sent = pl.pallas_call(
        pack_kernel,
        out_shape=jax.ShapeDtypeStruct((BANDS * PAY, BOX), BF16),
        in_specs=[vmem()] * 6,
        out_specs=vmem(),
        scratch_shapes=[
            pltpu.VMEM((BANDS * PAY, arrivals), BF16),
            pltpu.VMEM((BOX, arrivals), BF16),
        ],
        compiler_params=params(32),
        name="pack",
    )(
        values,
        tile.reshape(-1, 128),
        row.reshape(-1, 128),
        col.reshape(-1, 128),
        frac,
        place.reshape(2, 128),
    )
    came = lax.all_to_all(sent, "band", split_axis=0, concat_axis=0, tiled=True)
    groups = BANDS + EXTRA
    own = pl.pallas_call(
        regroup_kernel,
        out_shape=jax.ShapeDtypeStruct((groups * PAY, 128), BF16),
        in_specs=[vmem()],
        out_specs=vmem(),
        scratch_shapes=[
            pltpu.VMEM((groups * PAY, BANDS * BOX), BF16),
            pltpu.VMEM((128, BANDS * BOX), BF16),
        ],
        compiler_params=params(32),
        name="regroup",
    )(came)
    count = lax.axis_size("obs")
    chips = count // 2

    def along(value, steps):
        order = [(s, ((s // 2 + steps) % chips) * 2 + s % 2) for s in range(count)]
        return lax.ppermute(value, "obs", order)

    def across(value):
        return lax.ppermute(value, "obs", [(s, s ^ 1) for s in range(count)])

    mine = [own] + [along(own, steps) for steps in range(1, chips)]
    blocks = mine + [across(value) for value in mine]
    columns = LON // 2
    shape = jax.ShapeDtypeStruct
    return pl.pallas_call(
        sums_kernel,
        out_shape=(
            shape((columns, 256), BF16),
            shape((columns, 128), BF16),
            shape((368, 128), BF16),
            shape((8, 128), F32),
        ),
        in_specs=[pl.BlockSpec(memory_space=pltpu.SMEM)] + [vmem()] * len(blocks),
        out_specs=(vmem(),) * 4,
        scratch_shapes=[
            pltpu.VMEM((256, len(blocks) * 128), BF16),
            pltpu.VMEM((2 * HALF_PAD, len(blocks) * 128), BF16),
            pltpu.VMEM((2 * HALF_PAD * (BANDS + 1), 256), F32),
            pltpu.VMEM((columns, 256), F32),
            pltpu.VMEM((8, 128), jnp.int32),
            pltpu.SMEM((8, 128), jnp.int32),
            pltpu.SemaphoreType.DMA,
        ],
        compiler_params=params(32),
        name="sums",
    )(scale, *blocks)


def from_behind(value, axis, steps):
    count = lax.axis_size(axis)
    first, last = (max(0, -steps), min(count, count - steps))
    return lax.ppermute(value, axis, [(source, source + steps) for source in range(first, last)])


def general(
    obs_values,
    obs_tile,
    obs_row,
    obs_col,
    obs_frac,
    tile_place,
    length_scale,
    conv_weight,
    conv_bias,
):
    band_count = lax.axis_size("band")
    obs_count = lax.axis_size("obs")
    arrivals = obs_tile.shape[0]
    capacity = arrivals // 4
    channels = obs_values.shape[0]
    lat_dev = ROWS_DEV * obs_count
    tile_width = LON // band_count
    band_ids = jnp.arange(band_count, dtype=jnp.int32)
    owner_band = obs_tile % band_count
    within = obs_tile // band_count
    member = (owner_band[:, None] == band_ids[None, :]).astype(jnp.int32)
    slot_rank = jnp.sum(jnp.cumsum(member, axis=0) * member, axis=1) - 1
    target = owner_band * capacity + slot_rank
    payload = jnp.concatenate(
        [
            obs_values.astype(jnp.float32),
            (obs_row.astype(jnp.float32) + obs_frac[0])[None],
            (obs_col.astype(jnp.float32) + obs_frac[1])[None],
            within.astype(jnp.float32)[None],
        ],
        axis=0,
    )
    outbox = (
        jnp.zeros((channels + 3, band_count * capacity), jnp.float32).at[channels + 2].set(-1.0)
    )
    outbox = outbox.at[:, target].set(payload)
    arrived_obs = lax.all_to_all(
        outbox.reshape(channels + 3, band_count, capacity),
        "band",
        split_axis=1,
        concat_axis=1,
        tiled=True,
    )
    inv_lat = 0.5 / (length_scale[0] * length_scale[0])
    inv_lon = 0.5 / (length_scale[1] * length_scale[1])
    row_mid = jnp.arange(lat_dev, dtype=jnp.float32) + 0.5
    col_mid = jnp.arange(tile_width, dtype=jnp.float32) + 0.5
    tile_codes = band_ids.astype(jnp.float32)

    def accumulate(source, running):
        source_block = lax.dynamic_index_in_dim(arrived_obs, source, 1, keepdims=False)
        lat_at = source_block[channels]
        lon_at = source_block[channels + 1]
        slot_at = source_block[channels + 2]
        lat_diff = row_mid[:, None] - lat_at[None, :]
        lon_diff = col_mid[:, None] - lon_at[None, :]
        lat_weight = jnp.exp(-(lat_diff * lat_diff) * inv_lat)
        lon_weight = jnp.exp(-(lon_diff * lon_diff) * inv_lon)
        extended = jnp.concatenate(
            [source_block[:channels], jnp.ones((1, capacity), jnp.float32)], axis=0
        )
        left_factor = (
            (extended[:, None, :] * lat_weight[None])
            .astype(jnp.bfloat16)
            .reshape((channels + 1) * lat_dev, capacity)
        )
        tile_pick = (slot_at[None, :] == tile_codes[:, None]).astype(jnp.float32)
        right_factor = (
            (tile_pick[:, None, :] * lon_weight[None])
            .astype(jnp.bfloat16)
            .reshape(band_count * tile_width, capacity)
        )
        return running + lax.dot_general(
            left_factor, right_factor, (((1,), (1,)), ((), ())), preferred_element_type=jnp.float32
        )

    grid_sums = lax.fori_loop(
        0, band_count, accumulate, jnp.zeros(((channels + 1) * lat_dev, LON), jnp.float32)
    )
    grid_sums = grid_sums.reshape(channels + 1, lat_dev, band_count, tile_width)
    my_band = lax.axis_index("band")
    place_table = tile_place.reshape(band_count, band_count)
    bands_of = place_table // band_count
    blocks_of = place_table % band_count
    my_bands = lax.dynamic_index_in_dim(bands_of, my_band, 1, keepdims=False)
    send_order = jnp.sum(
        (my_bands[None, :] == band_ids[:, None]).astype(jnp.int32) * band_ids[None, :], axis=1
    )
    outgoing = jnp.take(grid_sums, send_order, axis=2)
    matched = (bands_of == my_band).astype(jnp.int32)
    block_of_source = jnp.sum(matched * blocks_of, axis=0)
    source_of_block = jnp.sum(
        (block_of_source[None, :] == band_ids[:, None]).astype(jnp.int32) * band_ids[None, :],
        axis=1,
    )
    arrived = lax.all_to_all(outgoing, "band", split_axis=2, concat_axis=2, tiled=True)
    placed = jnp.take(arrived, source_of_block, axis=2).reshape(channels + 1, lat_dev, LON)
    band_rows = lax.psum_scatter(placed, "obs", scatter_dimension=1, tiled=True)
    density = band_rows[channels]
    feature = jnp.concatenate(
        [band_rows[:channels] / jnp.maximum(density, 1.0)[None], jnp.log(1.0 + density)[None]],
        axis=0,
    ).astype(jnp.bfloat16)
    rim_lower = from_behind(feature[:, -2:, :], ("band", "obs"), 1)
    rim_upper = from_behind(feature[:, :1, :], ("band", "obs"), -1)
    stacked = jnp.concatenate([rim_lower, feature, rim_upper], axis=1)
    wrapped = jnp.concatenate([stacked[:, :, -2:], stacked, stacked[:, :, :2]], axis=2)
    conv_out = lax.conv_general_dilated(
        wrapped[None],
        conv_weight,
        (2, 2),
        "VALID",
        dimension_numbers=("NCHW", "HWIO", "NHWC"),
        preferred_element_type=jnp.float32,
    )[0]
    return (conv_out + conv_bias).astype(jnp.bfloat16)


def body(*args):
    *_, conv_weight, conv_bias = args
    feature, lower, upper, over = fast_features(*args[:7])
    lower = from_behind(lower, ("band", "obs"), 1)
    upper = from_behind(upper, ("band", "obs"), -1)

    def finish(feature, lower, upper, *args):
        *_, conv_weight, conv_bias = args
        columns = LON // 2
        return pl.pallas_call(
            conv_kernel,
            out_shape=jax.ShapeDtypeStruct((2, columns, 256), BF16),
            in_specs=[vmem()] * 5,
            out_specs=vmem(),
            scratch_shapes=[
                pltpu.VMEM((columns + 16, 512), F32),
                pltpu.VMEM((3, 512, 512), BF16),
            ],
            compiler_params=params(32),
            name="conv",
        )(feature, lower, upper, conv_weight, conv_bias.reshape(1, -1))

    def whole(feature, lower, upper, *args):
        return general(*args)

    return lax.cond(over[0, 0] > 0.0, whole, finish, feature, lower, upper, *args)


def solution(mesh):
    placed = (
        P(None, ("band", "obs")),
        P(("band", "obs")),
        P(("band", "obs")),
        P(("band", "obs")),
        P(None, ("band", "obs")),
        P(),
        P(),
        P(),
        P(),
    )
    return jax.shard_map(
        body, mesh=mesh, in_specs=placed, out_specs=P(("band", "obs"), None, None), check_vma=False
    )
```

```python
import functools

import jax
import jax.numpy as jnp
from jax import lax
from jax.experimental import pallas as pl
from jax.experimental.pallas import tpu as pltpu
from jax.sharding import PartitionSpec as P

LON = 1440
ROWS_DEV = 4
BANDS = 16
TQ = 90
HALF = TQ // 2
HALF_PAD = 48
BOX = 256
EXTRA = 8
HEAD = 4
ROW_CODE = 24
ROW_LAT = 25
ROW_LON = 28
ROW_NOTE = 31
PAY = 32
SLOTS = 8
LAT_BAND = 32
ROWS_IN = 7
TALL = 2 * HALF_PAD
LOG2E = 1.4426950408889634
F32 = jnp.float32
BF16 = jnp.bfloat16


def dot_nt(left, right):
    return lax.dot_general(left, right, (((1,), (1,)), ((), ())), preferred_element_type=F32)


def iota(shape, dim):
    return lax.broadcasted_iota(jnp.int32, shape, dim)


def ones_where(mask):
    return jnp.where(mask, 1.0, 0.0)


def ranks(member):
    chunks = len(member)
    rows = chunks * BANDS
    stacked = jnp.concatenate(member, axis=0).astype(BF16)
    before = ones_where(iota((BOX, BOX), 0) < iota((BOX, BOX), 1)).astype(BF16)
    at, of = iota((rows, rows), 0), iota((rows, rows), 1)
    earlier = ones_where(((of & 15) == (at & 15)) & ((of >> 4) < (at >> 4))).astype(BF16)
    inside = jnp.dot(stacked, before, preferred_element_type=F32)
    base = jnp.sum(jnp.dot(earlier, stacked, preferred_element_type=F32), axis=1, keepdims=True)
    place = inside + base
    return [
        jnp.sum(member[k] * place[k * BANDS : (k + 1) * BANDS], axis=0, keepdims=True)
        for k in range(chunks)
    ]


def bucket(payload, group, position, left_ref, right_ref, k):
    lanes = slice(k * BOX, (k + 1) * BOX)
    for g in range(left_ref.shape[0] // PAY):
        left_ref[g * PAY : (g + 1) * PAY, lanes] = jnp.where(group == g, payload, 0.0).astype(BF16)
    right_ref[:, lanes] = ones_where(iota((right_ref.shape[0], BOX), 0) == position).astype(BF16)


def split3(value):
    high = value.astype(BF16).astype(F32)
    rest = value - high
    middle = rest.astype(BF16).astype(F32)
    return high, middle, rest - middle


def pack_kernel(values_ref, tile_ref, row_ref, col_ref, frac_ref, place_ref, out_ref, left_ref, right_ref):
    chunks = tile_ref.shape[0] * 128 // BOX

    def wide(ref, k):
        return jnp.concatenate([ref[2 * k : 2 * k + 1, :], ref[2 * k + 1 : 2 * k + 2, :]], axis=1)

    table = jnp.broadcast_to(wide(place_ref, 0).astype(F32), (8, BOX)).astype(BF16)
    ones = jnp.ones((8, BOX), BF16)
    lines = iota((BOX, BOX), 0)
    eight = iota((8, BOX), 0)
    counts = jnp.zeros((8, BOX), F32)
    bands, blocks, member = [], [], []
    for k in range(chunks):
        tile_pick = ones_where(lines == wide(tile_ref, k)).astype(BF16)
        place = jnp.dot(table, tile_pick, preferred_element_type=F32)[0:1].astype(jnp.int32)
        counts = counts + dot_nt(ones, ones_where(lines == place).astype(BF16))
        bands.append(place >> 4)
        blocks.append(place & 15)
        member.append(ones_where(iota((BANDS, BOX), 0) == bands[k]))
    rank = ranks(member)
    for k in range(chunks):
        lanes = slice(k * BOX, (k + 1) * BOX)
        lat = split3(wide(row_ref, k).astype(F32) + frac_ref[0:1, lanes])
        lon = split3(wide(col_ref, k).astype(F32) + frac_ref[1:2, lanes])
        tail = jnp.zeros((8, BOX), F32)
        for at, line in enumerate([blocks[k].astype(F32) + 1.0, *lat, *lon]):
            tail = jnp.where(eight == at, line, tail)
        payload = jnp.concatenate([values_ref[:, lanes].astype(F32), tail], axis=0)
        bucket(payload, bands[k], rank[k].astype(jnp.int32), left_ref, right_ref, k)
    packed = dot_nt(left_ref[...], right_ref[...])
    line_of = iota((PAY, BOX), 0)
    for g in range(BANDS):
        rows = slice(g * PAY, (g + 1) * PAY)
        out_ref[rows, :] = jnp.where(line_of == ROW_NOTE, counts[0:1], packed[rows]).astype(BF16)


def regroup_kernel(in_ref, out_ref, left_ref, right_ref):
    chunks = in_ref.shape[0] // PAY
    codes, member, notes = [], [], []
    line_of = iota((PAY, BOX), 0)
    total = jnp.zeros((BANDS, 1), F32)
    for k in range(chunks):
        tail = in_ref[k * PAY + 16 : (k + 1) * PAY, :].astype(F32)
        codes.append(tail[ROW_CODE - 16 : ROW_CODE - 15].astype(jnp.int32) - 1)
        notes.append(tail[ROW_NOTE - 16 : ROW_NOTE - 15])
        member.append(ones_where(iota((BANDS, BOX), 0) == codes[k]))
        total = total + jnp.sum(member[k], axis=1, keepdims=True)
    rank = ranks(member)

    more = jnp.maximum(jnp.broadcast_to(total, (BANDS, 128)).astype(jnp.int32) - 1, 0) >> 7
    key = more * BANDS + (BANDS - 1 - iota((BANDS, 128), 0))
    leads = key == jnp.max(key, axis=0, keepdims=True)
    more = jnp.where(leads, jnp.maximum(more, HEAD), more)
    key = more * BANDS + (BANDS - 1 - iota((BANDS, 128), 0))
    more = more.astype(F32)
    first = jnp.zeros((BANDS, 128), F32)
    for g in range(BANDS):
        first = first + jnp.where(key[g : g + 1] > key, more[g : g + 1], 0.0)
    first = jnp.where(leads, 0.0, first)
    last = first + more
    first_wide = jnp.concatenate([first, first], axis=1)

    for k in range(chunks):
        payload = in_ref[k * PAY : (k + 1) * PAY, :].astype(F32)
        payload = jnp.where(line_of == ROW_CODE, 1.0, jnp.where(line_of == ROW_NOTE, 0.0, payload))
        place = rank[k].astype(jnp.int32)
        over = jnp.sum(member[k] * first_wide, axis=0, keepdims=True).astype(jnp.int32)
        group = jnp.where(place < 128, codes[k], BANDS - 1 + over + (place >> 7))
        group = jnp.where(codes[k] < 0, -1, group)
        bucket(payload, group, place & 127, left_ref, right_ref, k)
    moved = dot_nt(left_ref[...], right_ref[...])

    note = jnp.concatenate(notes, axis=0)
    of_band = ones_where((iota((BOX, 128), 0) >> 4) == iota((BOX, 128), 1)).astype(BF16)
    band_sums = jnp.dot(note.astype(BF16), of_band, preferred_element_type=F32)
    tile_sums = jnp.broadcast_to(jnp.sum(note, axis=0, keepdims=True), (BANDS, BOX)).astype(jnp.int32)
    tile_more = jnp.maximum(tile_sums - 1, 0) >> 7
    tile_more = jnp.where((iota((BANDS, BOX), 1) >> 4) == iota((BANDS, BOX), 0), tile_more, 0).astype(F32)
    most = jnp.max(tile_more, axis=1, keepdims=True)
    more_sums = jnp.sum(tile_more, axis=1, keepdims=True) + jnp.maximum(HEAD - most, 0.0)
    band_most = jnp.max(jnp.max(band_sums, axis=1, keepdims=True), axis=0, keepdims=True)
    more_most = jnp.max(more_sums, axis=0, keepdims=True)
    over = jnp.where((band_most > BOX - 1) | (more_most > EXTRA), 1.0, 0.0)

    narrow = iota((PAY, 128), 0)
    out_ref[0:PAY, :] = jnp.where(narrow == ROW_NOTE, over, moved[0:PAY]).astype(BF16)
    out_ref[PAY : BANDS * PAY, :] = moved[PAY : BANDS * PAY].astype(BF16)
    block_code = iota((BANDS, 128), 0).astype(F32) + 1.0
    for e in range(EXTRA):
        rows = slice((BANDS + e) * PAY, (BANDS + e + 1) * PAY)
        code = jnp.where((first <= e) & (last > e), block_code, 0.0)
        code = jnp.sum(code, axis=0, keepdims=True)
        out_ref[rows, :] = jnp.where(narrow == ROW_NOTE, code, moved[rows]).astype(BF16)


def sums_kernel(count, last, scale_ref, *refs):
    block_refs, refs = refs[:count], refs[count:]
    if last:
        *before_refs, feature_ref, edge_ref, over_ref = refs[:-7]
        left_ref, right_ref, codes_ref, codes_smem, sem, sums_ref, wide_ref = refs[-7:]
    else:
        sums_ref, over_ref, left_ref, right_ref, codes_ref, codes_smem, sem = refs
    shard = lax.axis_index("obs")
    scale = jnp.full((8, 128), 1.0, F32)
    lat_scale = (-0.5 * LOG2E) / (scale * scale_ref[0] * scale_ref[0])
    lon_scale = (-0.5 * LOG2E) / (scale * scale_ref[1] * scale_ref[1])
    lat_scale, lon_scale = lat_scale[0:1], lon_scale[0:1]
    row_mid = ((iota((8, 128), 0) + (shard * ROWS_DEV - 2)) & (LAT_BAND - 1)).astype(F32) + 0.5
    line = iota((2 * HALF_PAD, 128), 0)
    past = (line >= HALF_PAD).astype(jnp.int32)
    col_mid = (2 * (line - HALF_PAD * past) + past).astype(F32) + 0.5
    lane = iota((8, 128), 1)
    sub = iota((8, 128), 0)

    codes = jnp.zeros((8, 128), F32)
    for k in range(count):
        for e in range(EXTRA):
            at = (BANDS + e) * PAY + 16
            note = block_refs[k][at : at + 16, :].astype(F32)[15:16]
            codes = jnp.where((lane == e) & (sub == k), note, codes)
    codes_ref[...] = codes.astype(jnp.int32)
    copy = pltpu.make_async_copy(codes_ref, codes_smem, sem)
    copy.start()

    def factors(start, slot):
        for k in range(count):
            lanes = slice(k * 128, (k + 1) * 128)
            value = block_refs[k][pl.ds(start, PAY), :].astype(F32)
            tail = value[24:32]
            lat_at = tail[1:2] + tail[2:3] + tail[3:4]
            lon_at = tail[4:5] + tail[5:6] + tail[6:7]
            lat_diff = row_mid - lat_at
            lat_weight = jnp.exp2(lat_diff * lat_diff * lat_scale)
            lon_diff = col_mid - lon_at
            lon_weight = jnp.exp2(lon_diff * lon_diff * lon_scale)
            for r in range(ROWS_IN):
                left_ref[slot, r * PAY : (r + 1) * PAY, lanes] = (value * lat_weight[r : r + 1]).astype(BF16)
            right_ref[slot, :, lanes] = lon_weight.astype(BF16)

    slots = left_ref.shape[0]
    for slot in range(slots):
        left_ref[slot, ROWS_IN * PAY :, :] = jnp.zeros((PAY, count * 128), BF16)

    def main(p, carry):
        for slot in range(slots):
            at = p * slots + slot
            factors(pl.multiple_of(at * PAY, PAY), slot)
            start = pl.multiple_of((at + 1) * TALL, TALL)
            sums_ref[pl.ds(start, TALL), :] = dot_nt(right_ref[slot], left_ref[slot])
        return carry

    sums_ref[0:TALL, :] = jnp.zeros((TALL, 256), F32)
    lax.fori_loop(0, BANDS // slots, main, 0)

    copy.wait()
    used = jnp.int32(0)
    for e in range(HEAD, EXTRA):
        for k in range(count):
            used = jnp.where(codes_smem[k, e] > 0, e + 1 - HEAD, used)
    for e in range(HEAD):
        factors((BANDS + e) * PAY, e)
    for k in range(count):
        lanes = slice(k * 128, (k + 1) * 128)
        right = jnp.concatenate([right_ref[e, :, lanes] for e in range(HEAD)], axis=1)
        left = jnp.concatenate([left_ref[e, :, lanes] for e in range(HEAD)], axis=1)
        start = pl.multiple_of(codes_smem[k, 0] * TALL, TALL)
        sums_ref[pl.ds(start, TALL), :] += dot_nt(right, left)

    def extra(e, carry):
        factors(pl.multiple_of((BANDS + HEAD + e) * PAY, PAY), 0)
        for k in range(count):
            lanes = slice(k * 128, (k + 1) * 128)
            start = pl.multiple_of(codes_smem[k, HEAD + e] * TALL, TALL)
            sums_ref[pl.ds(start, TALL), :] += dot_nt(right_ref[0, :, lanes], left_ref[0, :, lanes])
        return carry

    lax.fori_loop(0, used, extra, 0)

    over = block_refs[0][16:PAY, :].astype(F32)[15:16]
    for k in range(1, count):
        over = jnp.maximum(over, block_refs[k][16:PAY, :].astype(F32)[15:16])
    over = jnp.broadcast_to(over, (8, 128))
    if not last:
        over_ref[...] = over
        return
    sums_before, overs_before = before_refs[0::2], before_refs[1::2]
    for ref in overs_before:
        over = jnp.maximum(over, ref[...])
    over_ref[...] = over

    channel = iota((TALL, 128), 1) & (PAY - 1)
    dense = iota((TALL, 128), 1) - channel + ROW_CODE
    for block in range(BANDS):
        rows = slice(block * HALF, (block + 1) * HALF)
        at = slice((block + 1) * TALL, (block + 2) * TALL)
        for half in range(2):
            lanes = slice(half * 128, (half + 1) * 128)
            total = sums_ref[at, lanes]
            for ref in sums_before:
                total = total + ref[at, lanes]
            density = jnp.take_along_axis(total, dense, axis=1)
            feature = total * (1.0 / jnp.maximum(density, 1.0))
            feature = jnp.where(channel < 24, feature, jnp.where(channel == 24, jnp.log(1.0 + density), 0.0))
            wide_ref[rows, lanes] = feature[0:HALF]
            wide_ref[rows, 256 + half * 128 : 256 + (half + 1) * 128] = feature[HALF_PAD : HALF_PAD + HALF]
    feature_ref[...] = wide_ref[...].astype(BF16)

    @pl.when(shard == 0)
    def _():
        edge_ref[...] = jnp.concatenate([wide_ref[:, 0:64], wide_ref[:, 256:320]], axis=1).astype(BF16)

    @pl.when(shard != 0)
    def _():
        edge_ref[...] = jnp.concatenate([wide_ref[:, 192:256], wide_ref[:, 448:512]], axis=1).astype(BF16)


def conv_kernel(feature_ref, edge_ref, weight_ref, bias_ref, out_ref, wide_ref, w_ref):
    columns = feature_ref.shape[0]
    shard = lax.axis_index("obs")
    w_ref[...] = jnp.zeros(w_ref.shape, BF16)
    channels = weight_ref.shape[2]
    zero = jnp.zeros((PAY - channels, 256), F32)
    for shift in range(3):
        for odd in range(2):
            if 2 * shift + odd < 5:
                for tap in range(5):
                    part = weight_ref[tap, 2 * shift + odd].astype(F32)
                    part = jnp.concatenate([part, zero], axis=0).astype(BF16)
                    for out_row in range(2):
                        at = odd * 256 + (tap + 2 * out_row) * PAY
                        w_ref[shift, at : at + PAY, out_row * 256 : (out_row + 1) * 256] = part

    border = 8
    inner = slice(border, border + columns)
    wide_ref[inner, :] = feature_ref[...].astype(F32)

    @pl.when(shard == 0)
    def _():
        edge = edge_ref[...].astype(F32)
        wide_ref[inner, 0:64] = edge[:, 0:64]
        wide_ref[inner, 256:320] = edge[:, 64:128]

    @pl.when(shard == lax.axis_size("obs") - 1)
    def _():
        edge = edge_ref[...].astype(F32)
        wide_ref[inner, 192:256] = edge[:, 0:64]
        wide_ref[inner, 448:512] = edge[:, 64:128]

    wide_ref[border - 1 : border, :] = wide_ref[border + columns - 1 : border + columns, :]
    wide_ref[border + columns : border + columns + 1, :] = wide_ref[border : border + 1, :]

    total = None
    for shift in range(3):
        start = border + shift - 1
        moved = wide_ref[start : start + columns, :].astype(BF16)
        part = jnp.dot(moved, w_ref[shift], preferred_element_type=F32)
        total = part if total is None else total + part
    bias = bias_ref[...]
    out_ref[0] = (total[:, 0:256] + bias).astype(BF16)
    out_ref[1] = (total[:, 256:512] + bias).astype(BF16)


def params(mib):
    return pltpu.CompilerParams(vmem_limit_bytes=mib * 2**20)


def vmem():
    return pl.BlockSpec(memory_space=pltpu.VMEM)


def fast_features(values, tile, row, col, frac, place, scale):
    arrivals = tile.shape[0]
    sent = pl.pallas_call(
        pack_kernel,
        out_shape=jax.ShapeDtypeStruct((BANDS * PAY, BOX), BF16),
        in_specs=[vmem()] * 6,
        out_specs=vmem(),
        scratch_shapes=[
            pltpu.VMEM((BANDS * PAY, arrivals), BF16),
            pltpu.VMEM((BOX, arrivals), BF16),
        ],
        compiler_params=params(32),
        name="pack",
    )(
        values,
        tile.reshape(-1, 128),
        row.reshape(-1, 128),
        col.reshape(-1, 128),
        frac,
        place.reshape(2, 128),
    )
    came = lax.all_to_all(sent, "band", split_axis=0, concat_axis=0, tiled=True)
    groups = BANDS + EXTRA
    own = pl.pallas_call(
        regroup_kernel,
        out_shape=jax.ShapeDtypeStruct((groups * PAY, 128), BF16),
        in_specs=[vmem()],
        out_specs=vmem(),
        scratch_shapes=[
            pltpu.VMEM((groups * PAY, BANDS * BOX), BF16),
            pltpu.VMEM((128, BANDS * BOX), BF16),
        ],
        compiler_params=params(32),
        name="regroup",
    )(came)
    count = lax.axis_size("obs")
    chips = count // 2

    def along(value, steps):
        order = [(s, ((s // 2 + steps) % chips) * 2 + s % 2) for s in range(count)]
        return lax.ppermute(value, "obs", order)

    def across(value):
        return lax.ppermute(value, "obs", [(s, s ^ 1) for s in range(count)])

    columns = LON // 2
    shape = jax.ShapeDtypeStruct

    def sums(blocks, before):
        last = before is not None
        tall = TALL * (BANDS + 1)
        if last:
            out_shape = (
                shape((columns, 512), BF16),
                shape((columns, 128), BF16),
                shape((8, 128), F32),
            )
        else:
            out_shape = (shape((tall, 256), F32), shape((8, 128), F32))
            before = ()
        slots = SLOTS
        scratch = [
            pltpu.VMEM((slots, 256, len(blocks) * 128), BF16),
            pltpu.VMEM((slots, TALL, len(blocks) * 128), BF16),
            pltpu.VMEM((8, 128), jnp.int32),
            pltpu.SMEM((8, 128), jnp.int32),
            pltpu.SemaphoreType.DMA,
        ]
        if last:
            scratch += [pltpu.VMEM((tall, 256), F32), pltpu.VMEM((columns, 512), F32)]
        return pl.pallas_call(
            functools.partial(sums_kernel, len(blocks), last),
            out_shape=out_shape,
            in_specs=[pl.BlockSpec(memory_space=pltpu.SMEM)] + [vmem()] * (len(blocks) + len(before)),
            out_specs=(vmem(),) * len(out_shape),
            scratch_shapes=scratch,
            compiler_params=params(32),
            cost_estimate=pl.CostEstimate(
                flops=len(blocks) * 1_200_000_000, bytes_accessed=len(blocks) * 200_000, transcendentals=0
            ),
            name="sums_last" if last else "sums",
        )(scale, *blocks, *before)

    far, after, ahead = (along(own, steps) for steps in (2, 1, -1))
    before = sums([own, across(own)], None)
    after, ahead, far, *before = lax.optimization_barrier((after, ahead, far, *before))
    there = [across(value) for value in (after, ahead, far)]
    return sums([after, ahead, far, *there], before)


def from_behind(value, axis, steps):
    count = lax.axis_size(axis)
    first, last = (max(0, -steps), min(count, count - steps))
    return lax.ppermute(value, axis, [(source, source + steps) for source in range(first, last)])


def general(
    obs_values,
    obs_tile,
    obs_row,
    obs_col,
    obs_frac,
    tile_place,
    length_scale,
    conv_weight,
    conv_bias,
):
    band_count = lax.axis_size("band")
    obs_count = lax.axis_size("obs")
    arrivals = obs_tile.shape[0]
    capacity = arrivals // 4
    channels = obs_values.shape[0]
    lat_dev = ROWS_DEV * obs_count
    tile_width = LON // band_count
    band_ids = jnp.arange(band_count, dtype=jnp.int32)
    owner_band = obs_tile % band_count
    within = obs_tile // band_count
    member = (owner_band[:, None] == band_ids[None, :]).astype(jnp.int32)
    slot_rank = jnp.sum(jnp.cumsum(member, axis=0) * member, axis=1) - 1
    target = owner_band * capacity + slot_rank
    payload = jnp.concatenate(
        [
            obs_values.astype(jnp.float32),
            (obs_row.astype(jnp.float32) + obs_frac[0])[None],
            (obs_col.astype(jnp.float32) + obs_frac[1])[None],
            within.astype(jnp.float32)[None],
        ],
        axis=0,
    )
    outbox = (
        jnp.zeros((channels + 3, band_count * capacity), jnp.float32).at[channels + 2].set(-1.0)
    )
    outbox = outbox.at[:, target].set(payload)
    arrived_obs = lax.all_to_all(
        outbox.reshape(channels + 3, band_count, capacity),
        "band",
        split_axis=1,
        concat_axis=1,
        tiled=True,
    )
    inv_lat = 0.5 / (length_scale[0] * length_scale[0])
    inv_lon = 0.5 / (length_scale[1] * length_scale[1])
    row_mid = jnp.arange(lat_dev, dtype=jnp.float32) + 0.5
    col_mid = jnp.arange(tile_width, dtype=jnp.float32) + 0.5
    tile_codes = band_ids.astype(jnp.float32)

    def accumulate(source, running):
        source_block = lax.dynamic_index_in_dim(arrived_obs, source, 1, keepdims=False)
        lat_at = source_block[channels]
        lon_at = source_block[channels + 1]
        slot_at = source_block[channels + 2]
        lat_diff = row_mid[:, None] - lat_at[None, :]
        lon_diff = col_mid[:, None] - lon_at[None, :]
        lat_weight = jnp.exp(-(lat_diff * lat_diff) * inv_lat)
        lon_weight = jnp.exp(-(lon_diff * lon_diff) * inv_lon)
        extended = jnp.concatenate(
            [source_block[:channels], jnp.ones((1, capacity), jnp.float32)], axis=0
        )
        left_factor = (
            (extended[:, None, :] * lat_weight[None])
            .astype(jnp.bfloat16)
            .reshape((channels + 1) * lat_dev, capacity)
        )
        tile_pick = (slot_at[None, :] == tile_codes[:, None]).astype(jnp.float32)
        right_factor = (
            (tile_pick[:, None, :] * lon_weight[None])
            .astype(jnp.bfloat16)
            .reshape(band_count * tile_width, capacity)
        )
        return running + lax.dot_general(
            left_factor, right_factor, (((1,), (1,)), ((), ())), preferred_element_type=jnp.float32
        )

    grid_sums = lax.fori_loop(
        0, band_count, accumulate, jnp.zeros(((channels + 1) * lat_dev, LON), jnp.float32)
    )
    grid_sums = grid_sums.reshape(channels + 1, lat_dev, band_count, tile_width)
    my_band = lax.axis_index("band")
    place_table = tile_place.reshape(band_count, band_count)
    bands_of = place_table // band_count
    blocks_of = place_table % band_count
    my_bands = lax.dynamic_index_in_dim(bands_of, my_band, 1, keepdims=False)
    send_order = jnp.sum(
        (my_bands[None, :] == band_ids[:, None]).astype(jnp.int32) * band_ids[None, :], axis=1
    )
    outgoing = jnp.take(grid_sums, send_order, axis=2)
    matched = (bands_of == my_band).astype(jnp.int32)
    block_of_source = jnp.sum(matched * blocks_of, axis=0)
    source_of_block = jnp.sum(
        (block_of_source[None, :] == band_ids[:, None]).astype(jnp.int32) * band_ids[None, :],
        axis=1,
    )
    arrived = lax.all_to_all(outgoing, "band", split_axis=2, concat_axis=2, tiled=True)
    placed = jnp.take(arrived, source_of_block, axis=2).reshape(channels + 1, lat_dev, LON)
    spread = lax.all_to_all(
        placed.reshape(channels + 1, obs_count, ROWS_DEV, LON), "obs", split_axis=1, concat_axis=1, tiled=True
    )
    band_rows = jnp.sum(spread, axis=1)
    density = band_rows[channels]
    feature = jnp.concatenate(
        [band_rows[:channels] / jnp.maximum(density, 1.0)[None], jnp.log(1.0 + density)[None]],
        axis=0,
    ).astype(jnp.bfloat16)
    rim_lower = from_behind(feature[:, -2:, :], ("band", "obs"), 1)
    rim_upper = from_behind(feature[:, :1, :], ("band", "obs"), -1)
    stacked = jnp.concatenate([rim_lower, feature, rim_upper], axis=1)
    wrapped = jnp.concatenate([stacked[:, :, -2:], stacked, stacked[:, :, :2]], axis=2)
    conv_out = lax.conv_general_dilated(
        wrapped[None],
        conv_weight,
        (2, 2),
        "VALID",
        dimension_numbers=("NCHW", "HWIO", "NHWC"),
        preferred_element_type=jnp.float32,
    )[0]
    return (conv_out + conv_bias).astype(jnp.bfloat16)


def body(*args):
    feature, edge, over = fast_features(*args[:7])
    bands, shards = lax.axis_size("band"), lax.axis_size("obs")
    down = [(band * shards, (band + 1) * shards) for band in range(bands - 1)]
    up = [(band * shards + shards - 1, band * shards - 1) for band in range(1, bands)]
    edge = lax.ppermute(edge, ("band", "obs"), down + up)

    def finish(feature, edge, *args):
        *_, conv_weight, conv_bias = args
        columns = LON // 2
        return pl.pallas_call(
            conv_kernel,
            out_shape=jax.ShapeDtypeStruct((2, columns, 256), BF16),
            in_specs=[vmem()] * 4,
            out_specs=vmem(),
            scratch_shapes=[
                pltpu.VMEM((columns + 16, 512), F32),
                pltpu.VMEM((3, 512, 512), BF16),
            ],
            compiler_params=params(32),
            name="conv",
        )(feature, edge, conv_weight, conv_bias.reshape(1, -1))

    def whole(feature, edge, *args):
        return general(*args)

    return lax.cond(over[0, 0] > 0.0, whole, finish, feature, edge, *args)


def solution(mesh):
    placed = (
        P(None, ("band", "obs")),
        P(("band", "obs")),
        P(("band", "obs")),
        P(("band", "obs")),
        P(None, ("band", "obs")),
        P(),
        P(),
        P(),
        P(),
    )
    return jax.shard_map(
        body, mesh=mesh, in_specs=placed, out_specs=P(("band", "obs"), None, None), check_vma=False
    )
```

```python
import functools

import jax
import jax.numpy as jnp
from jax import lax
from jax.experimental import pallas as pl
from jax.experimental.pallas import tpu as pltpu
from jax.sharding import PartitionSpec as P

LON = 1440
ROWS_DEV = 4
BANDS = 16
TQ = 90
HALF = TQ // 2
HALF_PAD = 48
BOX = 256
EXTRA = 7
HEAD = 4
ROW_CODE = 24
ROW_LAT = 25
ROW_LON = 28
ROW_NOTE = 31
PAY = 32
SLOTS = 8
LAT_BAND = 32
SENDS_DOWN = 4
SENDS_UP = 6
ROWS_IN = 7
TALL = 2 * HALF_PAD
LOG2E = 1.4426950408889634
F32 = jnp.float32
BF16 = jnp.bfloat16


def dot_nt(left, right):
    return lax.dot_general(left, right, (((1,), (1,)), ((), ())), preferred_element_type=F32)


def iota(shape, dim):
    return lax.broadcasted_iota(jnp.int32, shape, dim)


def ones_where(mask):
    return jnp.where(mask, 1.0, 0.0)


def ranks(member):
    chunks = len(member)
    rows = chunks * BANDS
    stacked = jnp.concatenate(member, axis=0).astype(BF16)
    before = ones_where(iota((BOX, BOX), 0) < iota((BOX, BOX), 1)).astype(BF16)
    at, of = iota((rows, rows), 0), iota((rows, rows), 1)
    earlier = ones_where(((of & 15) == (at & 15)) & ((of >> 4) < (at >> 4))).astype(BF16)
    inside = jnp.dot(stacked, before, preferred_element_type=F32)
    base = jnp.sum(jnp.dot(earlier, stacked, preferred_element_type=F32), axis=1, keepdims=True)
    place = inside + base
    return [
        jnp.sum(member[k] * place[k * BANDS : (k + 1) * BANDS], axis=0, keepdims=True)
        for k in range(chunks)
    ]


def bucket(payload, group, position, left_ref, right_ref, k):
    lanes = slice(k * BOX, (k + 1) * BOX)
    for g in range(left_ref.shape[0] // PAY):
        left_ref[g * PAY : (g + 1) * PAY, lanes] = jnp.where(group == g, payload, 0.0).astype(BF16)
    right_ref[:, lanes] = ones_where(iota((right_ref.shape[0], BOX), 0) == position).astype(BF16)


def split3(value):
    high = value.astype(BF16).astype(F32)
    rest = value - high
    middle = rest.astype(BF16).astype(F32)
    return high, middle, rest - middle


def pack_kernel(values_ref, tile_ref, row_ref, col_ref, frac_ref, place_ref, out_ref, left_ref, right_ref):
    chunks = tile_ref.shape[0] * 128 // BOX

    def wide(ref, k):
        return jnp.concatenate([ref[2 * k : 2 * k + 1, :], ref[2 * k + 1 : 2 * k + 2, :]], axis=1)

    table = jnp.concatenate(
        [jnp.broadcast_to(place_ref[h : h + 1, :].astype(F32), (128, 128)).T for h in range(2)], axis=0
    )
    lines = iota((BOX, 128), 0)
    eight = iota((8, BOX), 0)
    sixteen = iota((BANDS, BOX), 0)
    bands, blocks, member, within = [], [], [], []
    for k in range(chunks):
        place = [
            jnp.sum(jnp.where(lines == tile_ref[at : at + 1, :], table, 0.0), axis=0, keepdims=True)
            for at in (2 * k, 2 * k + 1)
        ]
        place = jnp.concatenate(place, axis=1).astype(jnp.int32)
        bands.append(place >> 4)
        blocks.append(place & 15)
        member.append(ones_where(sixteen == bands[k]))
        within.append(ones_where(sixteen == blocks[k]).astype(BF16))
    counts = dot_nt(jnp.concatenate(member, axis=1).astype(BF16), jnp.concatenate(within, axis=1))
    spread = ones_where((iota((BANDS, BOX), 1) & 15) == sixteen).astype(BF16)
    counts = jnp.dot(counts.astype(BF16), spread, preferred_element_type=F32)
    counts = jnp.sum(jnp.where((iota((BANDS, BOX), 1) >> 4) == sixteen, counts, 0.0), axis=0, keepdims=True)
    rank = ranks(member)
    for k in range(chunks):
        lanes = slice(k * BOX, (k + 1) * BOX)
        lat = split3(wide(row_ref, k).astype(F32) + frac_ref[0:1, lanes])
        lon = split3(wide(col_ref, k).astype(F32) + frac_ref[1:2, lanes])
        tail = jnp.zeros((8, BOX), F32)
        for at, line in enumerate([blocks[k].astype(F32) + 1.0, *lat, *lon]):
            tail = jnp.where(eight == at, line, tail)
        payload = jnp.concatenate([values_ref[:, lanes].astype(F32), tail], axis=0)
        bucket(payload, bands[k], rank[k].astype(jnp.int32), left_ref, right_ref, k)
    packed = dot_nt(left_ref[...], right_ref[...])
    line_of = iota((PAY, BOX), 0)
    for g in range(BANDS):
        rows = slice(g * PAY, (g + 1) * PAY)
        out_ref[rows, :] = jnp.where(line_of == ROW_NOTE, counts, packed[rows]).astype(BF16)


def regroup_kernel(in_ref, out_ref, left_ref, right_ref):
    chunks = in_ref.shape[0] // PAY
    codes, member, notes = [], [], []
    line_of = iota((PAY, BOX), 0)
    total = jnp.zeros((BANDS, 1), F32)
    for k in range(chunks):
        tail = in_ref[k * PAY + 16 : (k + 1) * PAY, :].astype(F32)
        codes.append(tail[ROW_CODE - 16 : ROW_CODE - 15].astype(jnp.int32) - 1)
        notes.append(tail[ROW_NOTE - 16 : ROW_NOTE - 15])
        member.append(ones_where(iota((BANDS, BOX), 0) == codes[k]))
        total = total + jnp.sum(member[k], axis=1, keepdims=True)
    rank = ranks(member)

    more = jnp.maximum(jnp.broadcast_to(total, (BANDS, 128)).astype(jnp.int32) - 1, 0) >> 7
    key = more * BANDS + (BANDS - 1 - iota((BANDS, 128), 0))
    leads = key == jnp.max(key, axis=0, keepdims=True)
    more = jnp.where(leads, jnp.maximum(more, HEAD), more)
    key = more * BANDS + (BANDS - 1 - iota((BANDS, 128), 0))
    more = more.astype(F32)
    first = jnp.zeros((BANDS, 128), F32)
    for g in range(BANDS):
        first = first + jnp.where(key[g : g + 1] > key, more[g : g + 1], 0.0)
    first = jnp.where(leads, 0.0, first)
    last = first + more
    first_wide = jnp.concatenate([first, first], axis=1)

    for k in range(chunks):
        payload = in_ref[k * PAY : (k + 1) * PAY, :].astype(F32)
        payload = jnp.where(line_of == ROW_CODE, 1.0, jnp.where(line_of == ROW_NOTE, 0.0, payload))
        place = rank[k].astype(jnp.int32)
        over = jnp.sum(member[k] * first_wide, axis=0, keepdims=True).astype(jnp.int32)
        group = jnp.where(place < 128, codes[k], BANDS - 1 + over + (place >> 7))
        group = jnp.where(codes[k] < 0, -1, group)
        bucket(payload, group >> 1, (place & 127) + ((group & 1) << 7), left_ref, right_ref, k)
    both = dot_nt(left_ref[...], right_ref[...])

    def moved(group):
        rows = slice((group >> 1) * PAY, (group >> 1) * PAY + PAY)
        return both[rows, 0:128] if group % 2 == 0 else both[rows, 128:256]


    note = jnp.concatenate(notes, axis=0)
    of_band = ones_where((iota((BOX, 128), 0) >> 4) == iota((BOX, 128), 1)).astype(BF16)
    band_sums = jnp.dot(note.astype(BF16), of_band, preferred_element_type=F32)
    tile_sums = jnp.broadcast_to(jnp.sum(note, axis=0, keepdims=True), (BANDS, BOX)).astype(jnp.int32)
    tile_more = jnp.maximum(tile_sums - 1, 0) >> 7
    tile_more = jnp.where((iota((BANDS, BOX), 1) >> 4) == iota((BANDS, BOX), 0), tile_more, 0).astype(F32)
    most = jnp.max(tile_more, axis=1, keepdims=True)
    more_sums = jnp.sum(tile_more, axis=1, keepdims=True) + jnp.maximum(HEAD - most, 0.0)
    band_most = jnp.max(jnp.max(band_sums, axis=1, keepdims=True), axis=0, keepdims=True)
    more_most = jnp.max(more_sums, axis=0, keepdims=True)
    over = jnp.where((band_most > BOX - 1) | (more_most > EXTRA), 1.0, 0.0)

    narrow = iota((PAY, 128), 0)
    out_ref[0:PAY, :] = jnp.where(narrow == ROW_NOTE, over, moved(0)).astype(BF16)
    for g in range(1, BANDS):
        out_ref[g * PAY : (g + 1) * PAY, :] = moved(g).astype(BF16)
    block_code = iota((BANDS, 128), 0).astype(F32) + 1.0
    for e in range(EXTRA):
        rows = slice((BANDS + e) * PAY, (BANDS + e + 1) * PAY)
        code = jnp.where((first <= e) & (last > e), block_code, 0.0)
        code = jnp.sum(code, axis=0, keepdims=True)
        out_ref[rows, :] = jnp.where(narrow == ROW_NOTE, code, moved(BANDS + e)).astype(BF16)


def sums_kernel(count, kind, scale_ref, *refs):
    shard = lax.axis_index("obs")
    if kind.startswith("edge"):

        @pl.when((shard == SENDS_DOWN) | (shard == SENDS_UP))
        def _():
            sums_work(count, kind, shard, scale_ref, *refs)

    else:
        sums_work(count, kind, shard, scale_ref, *refs)


def sums_work(count, kind, shard, scale_ref, *refs):
    last = kind == "last"
    block_refs, refs = refs[:count], refs[count:]
    if last:
        *before_refs, feature_ref, over_ref = refs[:-7]
        left_ref, right_ref, codes_ref, codes_smem, sem, sums_ref, wide_ref = refs[-7:]
    elif kind == "edge":
        before_ref, edge_ref, left_ref, right_ref, codes_ref, codes_smem, sem, sums_ref, wide_ref = refs
    elif kind == "edge_part":
        sums_ref, left_ref, right_ref, codes_ref, codes_smem, sem = refs
    else:
        sums_ref, over_ref, left_ref, right_ref, codes_ref, codes_smem, sem = refs
    wide = sums_ref.shape[1]
    if kind.startswith("edge"):
        rows_in, first_row = 2, jnp.where(shard == SENDS_DOWN, LAT_BAND - 2, 0)
    else:
        rows_in, first_row = ROWS_IN, shard * ROWS_DEV - 2
    scale = jnp.full((8, 128), 1.0, F32)
    lat_scale = (-0.5 * LOG2E) / (scale * scale_ref[0] * scale_ref[0])
    lon_scale = (-0.5 * LOG2E) / (scale * scale_ref[1] * scale_ref[1])
    lat_scale, lon_scale = lat_scale[0:1], lon_scale[0:1]
    row_mid = ((iota((8, 128), 0) + first_row) & (LAT_BAND - 1)).astype(F32) + 0.5
    line = iota((2 * HALF_PAD, 128), 0)
    past = (line >= HALF_PAD).astype(jnp.int32)
    col_mid = (2 * (line - HALF_PAD * past) + past).astype(F32) + 0.5
    lane = iota((8, 128), 1)
    sub = iota((8, 128), 0)

    codes = jnp.zeros((8, 128), F32)
    for k in range(count):
        for e in range(EXTRA):
            at = (BANDS + e) * PAY + 16
            note = block_refs[k][at : at + 16, :].astype(F32)[15:16]
            codes = jnp.where((lane == e) & (sub == k), note, codes)
    codes_ref[...] = codes.astype(jnp.int32)
    copy = pltpu.make_async_copy(codes_ref, codes_smem, sem)
    copy.start()

    def factors(start, slot):
        for k in range(count):
            lanes = slice(k * 128, (k + 1) * 128)
            value = block_refs[k][pl.ds(start, PAY), :].astype(F32)
            tail = value[24:32]
            lat_at = tail[1:2] + tail[2:3] + tail[3:4]
            lon_at = tail[4:5] + tail[5:6] + tail[6:7]
            lat_diff = row_mid - lat_at
            lat_weight = jnp.exp2(lat_diff * lat_diff * lat_scale)
            lon_diff = col_mid - lon_at
            lon_weight = jnp.exp2(lon_diff * lon_diff * lon_scale)
            for r in range(rows_in):
                left_ref[slot, r * PAY : (r + 1) * PAY, lanes] = (value * lat_weight[r : r + 1]).astype(BF16)
            right_ref[slot, :, lanes] = lon_weight.astype(BF16)

    slots = left_ref.shape[0]
    for slot in range(slots):
        left_ref[slot, rows_in * PAY :, :] = jnp.zeros((wide - rows_in * PAY, count * 128), BF16)

    def main(p, carry):
        for slot in range(slots):
            at = p * slots + slot
            factors(pl.multiple_of(at * PAY, PAY), slot)
            start = pl.multiple_of((at + 1) * TALL, TALL)
            sums_ref[pl.ds(start, TALL), :] = dot_nt(right_ref[slot], left_ref[slot])
        return carry

    sums_ref[0:TALL, :] = jnp.zeros((TALL, wide), F32)
    lax.fori_loop(0, BANDS // slots, main, 0)

    copy.wait()
    used = jnp.int32(0)
    for e in range(HEAD, EXTRA):
        for k in range(count):
            used = jnp.where(codes_smem[k, e] > 0, e + 1 - HEAD, used)
    for e in range(HEAD):
        factors((BANDS + e) * PAY, e)
    for k in range(count):
        lanes = slice(k * 128, (k + 1) * 128)
        right = jnp.concatenate([right_ref[e, :, lanes] for e in range(HEAD)], axis=1)
        left = jnp.concatenate([left_ref[e, :, lanes] for e in range(HEAD)], axis=1)
        start = pl.multiple_of(codes_smem[k, 0] * TALL, TALL)
        sums_ref[pl.ds(start, TALL), :] += dot_nt(right, left)

    def extra(e, carry):
        factors(pl.multiple_of((BANDS + HEAD + e) * PAY, PAY), 0)
        for k in range(count):
            lanes = slice(k * 128, (k + 1) * 128)
            start = pl.multiple_of(codes_smem[k, HEAD + e] * TALL, TALL)
            sums_ref[pl.ds(start, TALL), :] += dot_nt(right_ref[0, :, lanes], left_ref[0, :, lanes])
        return carry

    lax.fori_loop(0, used, extra, 0)

    channel = iota((TALL, 128), 1) & (PAY - 1)
    dense = iota((TALL, 128), 1) - channel + ROW_CODE

    def feature_of(total):
        density = jnp.take_along_axis(total, dense, axis=1)
        feature = total * (1.0 / jnp.maximum(density, 1.0))
        return jnp.where(channel < 24, feature, jnp.where(channel == 24, jnp.log(1.0 + density), 0.0))

    if kind == "edge_part":
        return
    if kind == "edge":
        for block in range(BANDS):
            rows = slice(block * HALF, (block + 1) * HALF)
            at = slice((block + 1) * TALL, (block + 2) * TALL)
            feature = feature_of(sums_ref[at, :] + before_ref[at, :])
            wide_ref[rows, 0:64] = feature[0:HALF, 0:64]
            wide_ref[rows, 64:128] = feature[HALF_PAD : HALF_PAD + HALF, 0:64]
        edge_ref[...] = wide_ref[...].astype(BF16)
        return

    over = block_refs[0][16:PAY, :].astype(F32)[15:16]
    for k in range(1, count):
        over = jnp.maximum(over, block_refs[k][16:PAY, :].astype(F32)[15:16])
    over = jnp.broadcast_to(over, (8, 128))
    if not last:
        over_ref[...] = over
        return
    sums_before, overs_before = before_refs[0::2], before_refs[1::2]
    for ref in overs_before:
        over = jnp.maximum(over, ref[...])
    over_ref[...] = over

    for block in range(BANDS):
        rows = slice(block * HALF, (block + 1) * HALF)
        at = slice((block + 1) * TALL, (block + 2) * TALL)
        for half in range(2):
            lanes = slice(half * 128, (half + 1) * 128)
            total = sums_ref[at, lanes]
            for ref in sums_before:
                total = total + ref[at, lanes]
            feature = feature_of(total)
            wide_ref[rows, lanes] = feature[0:HALF]
            wide_ref[rows, 256 + half * 128 : 256 + (half + 1) * 128] = feature[HALF_PAD : HALF_PAD + HALF]
    feature_ref[...] = wide_ref[...].astype(BF16)


def conv_kernel(feature_ref, edge_ref, weight_ref, bias_ref, out_ref, wide_ref, w_ref):
    columns = feature_ref.shape[0]
    shard = lax.axis_index("obs")
    w_ref[...] = jnp.zeros(w_ref.shape, BF16)
    channels = weight_ref.shape[2]
    zero = jnp.zeros((PAY - channels, 256), F32)
    for shift in range(3):
        for odd in range(2):
            if 2 * shift + odd < 5:
                for tap in range(5):
                    part = weight_ref[tap, 2 * shift + odd].astype(F32)
                    part = jnp.concatenate([part, zero], axis=0).astype(BF16)
                    for out_row in range(2):
                        at = odd * 256 + (tap + 2 * out_row) * PAY
                        w_ref[shift, at : at + PAY, out_row * 256 : (out_row + 1) * 256] = part

    border = 8
    inner = slice(border, border + columns)
    wide_ref[inner, :] = feature_ref[...].astype(F32)

    @pl.when(shard == 0)
    def _():
        edge = edge_ref[...].astype(F32)
        wide_ref[inner, 0:64] = edge[:, 0:64]
        wide_ref[inner, 256:320] = edge[:, 64:128]

    @pl.when(shard == lax.axis_size("obs") - 1)
    def _():
        edge = edge_ref[...].astype(F32)
        wide_ref[inner, 192:256] = edge[:, 0:64]
        wide_ref[inner, 448:512] = edge[:, 64:128]

    wide_ref[border - 1 : border, :] = wide_ref[border + columns - 1 : border + columns, :]
    wide_ref[border + columns : border + columns + 1, :] = wide_ref[border : border + 1, :]

    total = None
    for shift in range(3):
        start = border + shift - 1
        moved = wide_ref[start : start + columns, :].astype(BF16)
        part = jnp.dot(moved, w_ref[shift], preferred_element_type=F32)
        total = part if total is None else total + part
    bias = bias_ref[...]
    out_ref[0] = (total[:, 0:256] + bias).astype(BF16)
    out_ref[1] = (total[:, 256:512] + bias).astype(BF16)


def params(mib):
    return pltpu.CompilerParams(vmem_limit_bytes=mib * 2**20)


def vmem():
    return pl.BlockSpec(memory_space=pltpu.VMEM)


def fast_features(values, tile, row, col, frac, place, scale):
    arrivals = tile.shape[0]
    sent = pl.pallas_call(
        pack_kernel,
        out_shape=jax.ShapeDtypeStruct((BANDS * PAY, BOX), BF16),
        in_specs=[vmem()] * 6,
        out_specs=vmem(),
        scratch_shapes=[
            pltpu.VMEM((BANDS * PAY, arrivals), BF16),
            pltpu.VMEM((BOX, arrivals), BF16),
        ],
        compiler_params=params(32),
        name="pack",
    )(
        values,
        tile.reshape(-1, 128),
        row.reshape(-1, 128),
        col.reshape(-1, 128),
        frac,
        place.reshape(2, 128),
    )
    came = lax.all_to_all(sent, "band", split_axis=0, concat_axis=0, tiled=True)
    groups = BANDS + EXTRA
    own = pl.pallas_call(
        regroup_kernel,
        out_shape=jax.ShapeDtypeStruct((groups * PAY, 128), BF16),
        in_specs=[vmem()],
        out_specs=vmem(),
        scratch_shapes=[
            pltpu.VMEM(((groups + 1) // 2 * PAY, BANDS * BOX), BF16),
            pltpu.VMEM((BOX, BANDS * BOX), BF16),
        ],
        compiler_params=params(32),
        name="regroup",
    )(came)
    count = lax.axis_size("obs")
    chips = count // 2

    def along(value, steps):
        order = [(s, ((s // 2 + steps) % chips) * 2 + s % 2) for s in range(count)]
        return lax.ppermute(value, "obs", order)

    def across(value):
        return lax.ppermute(value, "obs", [(s, s ^ 1) for s in range(count)])

    columns = LON // 2
    shape = jax.ShapeDtypeStruct

    def sums(kind, blocks, before=()):
        tall = TALL * (BANDS + 1)
        wide = 128 if kind.startswith("edge") else 256
        slots = SLOTS
        scratch = [
            pltpu.VMEM((slots, wide, len(blocks) * 128), BF16),
            pltpu.VMEM((slots, TALL, len(blocks) * 128), BF16),
            pltpu.VMEM((8, 128), jnp.int32),
            pltpu.SMEM((8, 128), jnp.int32),
            pltpu.SemaphoreType.DMA,
        ]
        over = shape((8, 128), F32)
        if kind == "part":
            out_shape = (shape((tall, wide), F32), over)
        elif kind == "edge_part":
            out_shape = (shape((tall, wide), F32),)
        elif kind == "edge":
            out_shape = (shape((columns, 128), BF16),)
            scratch += [pltpu.VMEM((tall, wide), F32), pltpu.VMEM((columns, 128), F32)]
        else:
            out_shape = (shape((columns, 512), BF16), over)
            scratch += [pltpu.VMEM((tall, wide), F32), pltpu.VMEM((columns, 512), F32)]
        return pl.pallas_call(
            functools.partial(sums_kernel, len(blocks), kind),
            out_shape=out_shape,
            in_specs=[pl.BlockSpec(memory_space=pltpu.SMEM)] + [vmem()] * (len(blocks) + len(before)),
            out_specs=(vmem(),) * len(out_shape),
            scratch_shapes=scratch,
            compiler_params=params(32),
            cost_estimate=pl.CostEstimate(
                flops=len(blocks) * 1_200_000_000, bytes_accessed=len(blocks) * 200_000, transcendentals=0
            ),
            name=kind + "_sums",
        )(scale, *blocks, *before)

    far, after, ahead = (along(own, steps) for steps in (2, 1, -1))
    near = [own, across(own)]
    before = [*sums("part", near), *sums("edge_part", near)]
    after, ahead, far, *before = lax.optimization_barrier((after, ahead, far, *before))
    there = [after, ahead, far] + [across(value) for value in (after, ahead, far)]
    *before, edge_before = before
    (edge,) = sums("edge", there, [edge_before])
    edge, *there = lax.optimization_barrier((edge, *there))
    bands = lax.axis_size("band")
    down = [(band * count + SENDS_DOWN, (band + 1) * count) for band in range(bands - 1)]
    up = [(band * count + SENDS_UP, band * count - 1) for band in range(1, bands)]
    edge = lax.ppermute(edge, ("band", "obs"), down + up)
    feature, over = sums("last", there, before)
    return feature, edge, over


def from_behind(value, axis, steps):
    count = lax.axis_size(axis)
    first, last = (max(0, -steps), min(count, count - steps))
    return lax.ppermute(value, axis, [(source, source + steps) for source in range(first, last)])


def general(
    obs_values,
    obs_tile,
    obs_row,
    obs_col,
    obs_frac,
    tile_place,
    length_scale,
    conv_weight,
    conv_bias,
):
    band_count = lax.axis_size("band")
    obs_count = lax.axis_size("obs")
    arrivals = obs_tile.shape[0]
    capacity = arrivals // 4
    channels = obs_values.shape[0]
    lat_dev = ROWS_DEV * obs_count
    tile_width = LON // band_count
    band_ids = jnp.arange(band_count, dtype=jnp.int32)
    owner_band = obs_tile % band_count
    within = obs_tile // band_count
    member = (owner_band[:, None] == band_ids[None, :]).astype(jnp.int32)
    slot_rank = jnp.sum(jnp.cumsum(member, axis=0) * member, axis=1) - 1
    target = owner_band * capacity + slot_rank
    payload = jnp.concatenate(
        [
            obs_values.astype(jnp.float32),
            (obs_row.astype(jnp.float32) + obs_frac[0])[None],
            (obs_col.astype(jnp.float32) + obs_frac[1])[None],
            within.astype(jnp.float32)[None],
        ],
        axis=0,
    )
    outbox = (
        jnp.zeros((channels + 3, band_count * capacity), jnp.float32).at[channels + 2].set(-1.0)
    )
    outbox = outbox.at[:, target].set(payload)
    arrived_obs = lax.all_to_all(
        outbox.reshape(channels + 3, band_count, capacity),
        "band",
        split_axis=1,
        concat_axis=1,
        tiled=True,
    )
    inv_lat = 0.5 / (length_scale[0] * length_scale[0])
    inv_lon = 0.5 / (length_scale[1] * length_scale[1])
    row_mid = jnp.arange(lat_dev, dtype=jnp.float32) + 0.5
    col_mid = jnp.arange(tile_width, dtype=jnp.float32) + 0.5
    tile_codes = band_ids.astype(jnp.float32)

    def accumulate(source, running):
        source_block = lax.dynamic_index_in_dim(arrived_obs, source, 1, keepdims=False)
        lat_at = source_block[channels]
        lon_at = source_block[channels + 1]
        slot_at = source_block[channels + 2]
        lat_diff = row_mid[:, None] - lat_at[None, :]
        lon_diff = col_mid[:, None] - lon_at[None, :]
        lat_weight = jnp.exp(-(lat_diff * lat_diff) * inv_lat)
        lon_weight = jnp.exp(-(lon_diff * lon_diff) * inv_lon)
        extended = jnp.concatenate(
            [source_block[:channels], jnp.ones((1, capacity), jnp.float32)], axis=0
        )
        left_factor = (
            (extended[:, None, :] * lat_weight[None])
            .astype(jnp.bfloat16)
            .reshape((channels + 1) * lat_dev, capacity)
        )
        tile_pick = (slot_at[None, :] == tile_codes[:, None]).astype(jnp.float32)
        right_factor = (
            (tile_pick[:, None, :] * lon_weight[None])
            .astype(jnp.bfloat16)
            .reshape(band_count * tile_width, capacity)
        )
        return running + lax.dot_general(
            left_factor, right_factor, (((1,), (1,)), ((), ())), preferred_element_type=jnp.float32
        )

    grid_sums = lax.fori_loop(
        0, band_count, accumulate, jnp.zeros(((channels + 1) * lat_dev, LON), jnp.float32)
    )
    grid_sums = grid_sums.reshape(channels + 1, lat_dev, band_count, tile_width)
    my_band = lax.axis_index("band")
    place_table = tile_place.reshape(band_count, band_count)
    bands_of = place_table // band_count
    blocks_of = place_table % band_count
    my_bands = lax.dynamic_index_in_dim(bands_of, my_band, 1, keepdims=False)
    send_order = jnp.sum(
        (my_bands[None, :] == band_ids[:, None]).astype(jnp.int32) * band_ids[None, :], axis=1
    )
    outgoing = jnp.take(grid_sums, send_order, axis=2)
    matched = (bands_of == my_band).astype(jnp.int32)
    block_of_source = jnp.sum(matched * blocks_of, axis=0)
    source_of_block = jnp.sum(
        (block_of_source[None, :] == band_ids[:, None]).astype(jnp.int32) * band_ids[None, :],
        axis=1,
    )
    arrived = lax.all_to_all(outgoing, "band", split_axis=2, concat_axis=2, tiled=True)
    placed = jnp.take(arrived, source_of_block, axis=2).reshape(channels + 1, lat_dev, LON)
    spread = lax.all_to_all(
        placed.reshape(channels + 1, obs_count, ROWS_DEV, LON), "obs", split_axis=1, concat_axis=1, tiled=True
    )
    band_rows = jnp.sum(spread, axis=1)
    density = band_rows[channels]
    feature = jnp.concatenate(
        [band_rows[:channels] / jnp.maximum(density, 1.0)[None], jnp.log(1.0 + density)[None]],
        axis=0,
    ).astype(jnp.bfloat16)
    rim_lower = from_behind(feature[:, -2:, :], ("band", "obs"), 1)
    rim_upper = from_behind(feature[:, :1, :], ("band", "obs"), -1)
    stacked = jnp.concatenate([rim_lower, feature, rim_upper], axis=1)
    wrapped = jnp.concatenate([stacked[:, :, -2:], stacked, stacked[:, :, :2]], axis=2)
    conv_out = lax.conv_general_dilated(
        wrapped[None],
        conv_weight,
        (2, 2),
        "VALID",
        dimension_numbers=("NCHW", "HWIO", "NHWC"),
        preferred_element_type=jnp.float32,
    )[0]
    return (conv_out + conv_bias).astype(jnp.bfloat16)


def body(*args):
    feature, edge, over = fast_features(*args[:7])
    def finish(feature, edge, *args):
        *_, conv_weight, conv_bias = args
        columns = LON // 2
        return pl.pallas_call(
            conv_kernel,
            out_shape=jax.ShapeDtypeStruct((2, columns, 256), BF16),
            in_specs=[vmem()] * 4,
            out_specs=vmem(),
            scratch_shapes=[
                pltpu.VMEM((columns + 16, 512), F32),
                pltpu.VMEM((3, 512, 512), BF16),
            ],
            compiler_params=params(32),
            name="conv",
        )(feature, edge, conv_weight, conv_bias.reshape(1, -1))

    def whole(feature, edge, *args):
        return general(*args)

    return lax.cond(over[0, 0] > 0.0, whole, finish, feature, edge, *args)


def solution(mesh):
    placed = (
        P(None, ("band", "obs")),
        P(("band", "obs")),
        P(("band", "obs")),
        P(("band", "obs")),
        P(None, ("band", "obs")),
        P(),
        P(),
        P(),
        P(),
    )
    return jax.shard_map(
        body, mesh=mesh, in_specs=placed, out_specs=P(("band", "obs"), None, None), check_vma=False
    )
```

```python
import functools

import jax
import jax.numpy as jnp
from jax import lax
from jax.experimental import pallas as pl
from jax.experimental.pallas import tpu as pltpu
from jax.sharding import PartitionSpec as P

LON = 1440
ROWS_DEV = 4
BANDS = 16
TQ = 90
HALF = TQ // 2
HALF_PAD = 48
BOX = 256
EXTRA = 7
HEAD = 4
ROW_CODE = 24
ROW_LAT = 25
ROW_LON = 28
ROW_NOTE = 31
PAY = 32
SLOTS = 8
LAT_BAND = 32
BORDER = 8
SENDS_DOWN = 4
SENDS_UP = 6
ROWS_IN = 7
TALL = 2 * HALF_PAD
LOG2E = 1.4426950408889634
F32 = jnp.float32
BF16 = jnp.bfloat16


def dot_nt(left, right):
    return lax.dot_general(left, right, (((1,), (1,)), ((), ())), preferred_element_type=F32)


def iota(shape, dim):
    return lax.broadcasted_iota(jnp.int32, shape, dim)


def ones_where(mask):
    return jnp.where(mask, 1.0, 0.0)


def ranks(member):
    chunks = len(member)
    rows = chunks * BANDS
    stacked = jnp.concatenate(member, axis=0).astype(BF16)
    before = ones_where(iota((BOX, BOX), 0) < iota((BOX, BOX), 1)).astype(BF16)
    at, of = iota((rows, rows), 0), iota((rows, rows), 1)
    earlier = ones_where(((of & 15) == (at & 15)) & ((of >> 4) < (at >> 4))).astype(BF16)
    inside = jnp.dot(stacked, before, preferred_element_type=F32)
    base = jnp.sum(jnp.dot(earlier, stacked, preferred_element_type=F32), axis=1, keepdims=True)
    place = inside + base
    return [
        jnp.sum(member[k] * place[k * BANDS : (k + 1) * BANDS], axis=0, keepdims=True)
        for k in range(chunks)
    ]


def bucket(payload, group, position, left_ref, right_ref, k):
    lanes = slice(k * BOX, (k + 1) * BOX)
    for g in range(left_ref.shape[0] // PAY):
        left_ref[g * PAY : (g + 1) * PAY, lanes] = jnp.where(group == g, payload, 0.0).astype(BF16)
    right_ref[:, lanes] = ones_where(iota((right_ref.shape[0], BOX), 0) == position).astype(BF16)


def split3(value):
    high = value.astype(BF16).astype(F32)
    rest = value - high
    middle = rest.astype(BF16).astype(F32)
    return high, middle, rest - middle


def pack_kernel(values_ref, tile_ref, row_ref, col_ref, frac_ref, place_ref, out_ref, left_ref, right_ref):
    chunks = tile_ref.shape[0] * 128 // BOX

    def wide(ref, k):
        return jnp.concatenate([ref[2 * k : 2 * k + 1, :], ref[2 * k + 1 : 2 * k + 2, :]], axis=1)

    table = jnp.concatenate(
        [jnp.broadcast_to(place_ref[h : h + 1, :].astype(F32), (128, 128)).T for h in range(2)], axis=0
    )
    lines = iota((BOX, 128), 0)
    eight = iota((8, BOX), 0)
    sixteen = iota((BANDS, BOX), 0)
    bands, blocks, member, within = [], [], [], []
    for k in range(chunks):
        place = [
            jnp.sum(jnp.where(lines == tile_ref[at : at + 1, :], table, 0.0), axis=0, keepdims=True)
            for at in (2 * k, 2 * k + 1)
        ]
        place = jnp.concatenate(place, axis=1).astype(jnp.int32)
        bands.append(place >> 4)
        blocks.append(place & 15)
        member.append(ones_where(sixteen == bands[k]))
        within.append(ones_where(sixteen == blocks[k]).astype(BF16))
    counts = dot_nt(jnp.concatenate(member, axis=1).astype(BF16), jnp.concatenate(within, axis=1))
    spread = ones_where((iota((BANDS, BOX), 1) & 15) == sixteen).astype(BF16)
    counts = jnp.dot(counts.astype(BF16), spread, preferred_element_type=F32)
    counts = jnp.sum(jnp.where((iota((BANDS, BOX), 1) >> 4) == sixteen, counts, 0.0), axis=0, keepdims=True)
    rank = ranks(member)
    for k in range(chunks):
        lanes = slice(k * BOX, (k + 1) * BOX)
        lat = split3(wide(row_ref, k).astype(F32) + frac_ref[0:1, lanes])
        lon = split3(wide(col_ref, k).astype(F32) + frac_ref[1:2, lanes])
        tail = jnp.zeros((8, BOX), F32)
        for at, line in enumerate([blocks[k].astype(F32) + 1.0, *lat, *lon]):
            tail = jnp.where(eight == at, line, tail)
        payload = jnp.concatenate([values_ref[:, lanes].astype(F32), tail], axis=0)
        bucket(payload, bands[k], rank[k].astype(jnp.int32), left_ref, right_ref, k)
    packed = dot_nt(left_ref[...], right_ref[...])
    line_of = iota((PAY, BOX), 0)
    for g in range(BANDS):
        rows = slice(g * PAY, (g + 1) * PAY)
        out_ref[rows, :] = jnp.where(line_of == ROW_NOTE, counts, packed[rows]).astype(BF16)


def regroup_kernel(in_ref, out_ref, left_ref, right_ref):
    chunks = in_ref.shape[0] // PAY
    codes, member, notes = [], [], []
    line_of = iota((PAY, BOX), 0)
    total = jnp.zeros((BANDS, 1), F32)
    for k in range(chunks):
        tail = in_ref[k * PAY + 16 : (k + 1) * PAY, :].astype(F32)
        codes.append(tail[ROW_CODE - 16 : ROW_CODE - 15].astype(jnp.int32) - 1)
        notes.append(tail[ROW_NOTE - 16 : ROW_NOTE - 15])
        member.append(ones_where(iota((BANDS, BOX), 0) == codes[k]))
        total = total + jnp.sum(member[k], axis=1, keepdims=True)
    rank = ranks(member)

    more = jnp.maximum(jnp.broadcast_to(total, (BANDS, 128)).astype(jnp.int32) - 1, 0) >> 7
    key = more * BANDS + (BANDS - 1 - iota((BANDS, 128), 0))
    leads = key == jnp.max(key, axis=0, keepdims=True)
    more = jnp.where(leads, jnp.maximum(more, HEAD), more)
    key = more * BANDS + (BANDS - 1 - iota((BANDS, 128), 0))
    more = more.astype(F32)
    first = jnp.zeros((BANDS, 128), F32)
    for g in range(BANDS):
        first = first + jnp.where(key[g : g + 1] > key, more[g : g + 1], 0.0)
    first = jnp.where(leads, 0.0, first)
    last = first + more
    first_wide = jnp.concatenate([first, first], axis=1)

    for k in range(chunks):
        payload = in_ref[k * PAY : (k + 1) * PAY, :].astype(F32)
        payload = jnp.where(line_of == ROW_CODE, 1.0, jnp.where(line_of == ROW_NOTE, 0.0, payload))
        place = rank[k].astype(jnp.int32)
        over = jnp.sum(member[k] * first_wide, axis=0, keepdims=True).astype(jnp.int32)
        group = jnp.where(place < 128, codes[k], BANDS - 1 + over + (place >> 7))
        group = jnp.where(codes[k] < 0, -1, group)
        bucket(payload, group >> 1, (place & 127) + ((group & 1) << 7), left_ref, right_ref, k)
    both = dot_nt(left_ref[...], right_ref[...])

    def moved(group):
        rows = slice((group >> 1) * PAY, (group >> 1) * PAY + PAY)
        return both[rows, 0:128] if group % 2 == 0 else both[rows, 128:256]


    note = jnp.concatenate(notes, axis=0)
    of_band = ones_where((iota((BOX, 128), 0) >> 4) == iota((BOX, 128), 1)).astype(BF16)
    band_sums = jnp.dot(note.astype(BF16), of_band, preferred_element_type=F32)
    tile_sums = jnp.broadcast_to(jnp.sum(note, axis=0, keepdims=True), (BANDS, BOX)).astype(jnp.int32)
    tile_more = jnp.maximum(tile_sums - 1, 0) >> 7
    tile_more = jnp.where((iota((BANDS, BOX), 1) >> 4) == iota((BANDS, BOX), 0), tile_more, 0).astype(F32)
    most = jnp.max(tile_more, axis=1, keepdims=True)
    more_sums = jnp.sum(tile_more, axis=1, keepdims=True) + jnp.maximum(HEAD - most, 0.0)
    band_most = jnp.max(jnp.max(band_sums, axis=1, keepdims=True), axis=0, keepdims=True)
    more_most = jnp.max(more_sums, axis=0, keepdims=True)
    over = jnp.where((band_most > BOX - 1) | (more_most > EXTRA), 1.0, 0.0)

    narrow = iota((PAY, 128), 0)
    out_ref[0:PAY, :] = jnp.where(narrow == ROW_NOTE, over, moved(0)).astype(BF16)
    for g in range(1, BANDS):
        out_ref[g * PAY : (g + 1) * PAY, :] = moved(g).astype(BF16)
    block_code = iota((BANDS, 128), 0).astype(F32) + 1.0
    for e in range(EXTRA):
        rows = slice((BANDS + e) * PAY, (BANDS + e + 1) * PAY)
        code = jnp.where((first <= e) & (last > e), block_code, 0.0)
        code = jnp.sum(code, axis=0, keepdims=True)
        out_ref[rows, :] = jnp.where(narrow == ROW_NOTE, code, moved(BANDS + e)).astype(BF16)


def sums_kernel(count, kind, scale_ref, *refs):
    shard = lax.axis_index("obs")
    if kind.startswith("edge"):

        @pl.when((shard == SENDS_DOWN) | (shard == SENDS_UP))
        def _():
            sums_work(count, kind, shard, scale_ref, *refs)

    else:
        sums_work(count, kind, shard, scale_ref, *refs)


def sums_work(count, kind, shard, scale_ref, *refs):
    last = kind == "last"
    block_refs, refs = refs[:count], refs[count:]
    if last:
        *before_refs, feature_ref, over_ref = refs[:-7]
        left_ref, right_ref, codes_ref, codes_smem, sem, sums_ref, wide_ref = refs[-7:]
    elif kind == "edge":
        before_ref, edge_ref, left_ref, right_ref, codes_ref, codes_smem, sem, sums_ref, wide_ref = refs
    elif kind == "edge_part":
        sums_ref, left_ref, right_ref, codes_ref, codes_smem, sem = refs
    else:
        sums_ref, over_ref, left_ref, right_ref, codes_ref, codes_smem, sem = refs
    wide = sums_ref.shape[1]
    if kind.startswith("edge"):
        rows_in, first_row = 2, jnp.where(shard == SENDS_DOWN, LAT_BAND - 2, 0)
    else:
        rows_in, first_row = ROWS_IN, shard * ROWS_DEV - 2
    scale = jnp.full((8, 128), 1.0, F32)
    lat_scale = (-0.5 * LOG2E) / (scale * scale_ref[0] * scale_ref[0])
    lon_scale = (-0.5 * LOG2E) / (scale * scale_ref[1] * scale_ref[1])
    lat_scale, lon_scale = lat_scale[0:1], lon_scale[0:1]
    row_mid = ((iota((8, 128), 0) + first_row) & (LAT_BAND - 1)).astype(F32) + 0.5
    line = iota((2 * HALF_PAD, 128), 0)
    past = (line >= HALF_PAD).astype(jnp.int32)
    col_mid = (2 * (line - HALF_PAD * past) + past).astype(F32) + 0.5
    lane = iota((8, 128), 1)
    sub = iota((8, 128), 0)

    codes = jnp.zeros((8, 128), F32)
    for k in range(count):
        for e in range(EXTRA):
            at = (BANDS + e) * PAY + 16
            note = block_refs[k][at : at + 16, :].astype(F32)[15:16]
            codes = jnp.where((lane == e) & (sub == k), note, codes)
    codes_ref[...] = codes.astype(jnp.int32)
    copy = pltpu.make_async_copy(codes_ref, codes_smem, sem)
    copy.start()

    def factors(start, slot):
        for k in range(count):
            lanes = slice(k * 128, (k + 1) * 128)
            value = block_refs[k][pl.ds(start, PAY), :].astype(F32)
            tail = value[24:32]
            lat_at = tail[1:2] + tail[2:3] + tail[3:4]
            lon_at = tail[4:5] + tail[5:6] + tail[6:7]
            lat_diff = row_mid - lat_at
            lat_weight = jnp.exp2(lat_diff * lat_diff * lat_scale)
            lon_diff = col_mid - lon_at
            lon_weight = jnp.exp2(lon_diff * lon_diff * lon_scale)
            for r in range(rows_in):
                left_ref[slot, r * PAY : (r + 1) * PAY, lanes] = (value * lat_weight[r : r + 1]).astype(BF16)
            right_ref[slot, :, lanes] = lon_weight.astype(BF16)

    slots = left_ref.shape[0]
    for slot in range(slots):
        left_ref[slot, rows_in * PAY :, :] = jnp.zeros((wide - rows_in * PAY, count * 128), BF16)

    def main(p, carry):
        for slot in range(slots):
            at = p * slots + slot
            factors(pl.multiple_of(at * PAY, PAY), slot)
            start = pl.multiple_of((at + 1) * TALL, TALL)
            sums_ref[pl.ds(start, TALL), :] = dot_nt(right_ref[slot], left_ref[slot])
        return carry

    sums_ref[0:TALL, :] = jnp.zeros((TALL, wide), F32)
    lax.fori_loop(0, BANDS // slots, main, 0)

    copy.wait()
    used = jnp.int32(0)
    for e in range(HEAD, EXTRA):
        for k in range(count):
            used = jnp.where(codes_smem[k, e] > 0, e + 1 - HEAD, used)
    for e in range(HEAD):
        factors((BANDS + e) * PAY, e)
    for k in range(count):
        lanes = slice(k * 128, (k + 1) * 128)
        right = jnp.concatenate([right_ref[e, :, lanes] for e in range(HEAD)], axis=1)
        left = jnp.concatenate([left_ref[e, :, lanes] for e in range(HEAD)], axis=1)
        start = pl.multiple_of(codes_smem[k, 0] * TALL, TALL)
        sums_ref[pl.ds(start, TALL), :] += dot_nt(right, left)

    def extra(e, carry):
        factors(pl.multiple_of((BANDS + HEAD + e) * PAY, PAY), 0)
        for k in range(count):
            lanes = slice(k * 128, (k + 1) * 128)
            start = pl.multiple_of(codes_smem[k, HEAD + e] * TALL, TALL)
            sums_ref[pl.ds(start, TALL), :] += dot_nt(right_ref[0, :, lanes], left_ref[0, :, lanes])
        return carry

    lax.fori_loop(0, used, extra, 0)

    channel = iota((TALL, 128), 1) & (PAY - 1)
    dense = iota((TALL, 128), 1) - channel + ROW_CODE

    def feature_of(total):
        density = jnp.take_along_axis(total, dense, axis=1)
        feature = total * (1.0 / jnp.maximum(density, 1.0))
        return jnp.where(channel < 24, feature, jnp.where(channel == 24, jnp.log(1.0 + density), 0.0))

    if kind == "edge_part":
        return
    if kind == "edge":
        for block in range(BANDS):
            rows = slice(block * HALF, (block + 1) * HALF)
            at = slice((block + 1) * TALL, (block + 2) * TALL)
            feature = feature_of(sums_ref[at, :] + before_ref[at, :])
            wide_ref[rows, 0:64] = feature[0:HALF, 0:64]
            wide_ref[rows, 64:128] = feature[HALF_PAD : HALF_PAD + HALF, 0:64]
        edge_ref[...] = wide_ref[...].astype(BF16)
        return

    over = block_refs[0][16:PAY, :].astype(F32)[15:16]
    for k in range(1, count):
        over = jnp.maximum(over, block_refs[k][16:PAY, :].astype(F32)[15:16])
    over = jnp.broadcast_to(over, (8, 128))
    if not last:
        over_ref[...] = over
        return
    sums_before, overs_before = before_refs[0::2], before_refs[1::2]
    for ref in overs_before:
        over = jnp.maximum(over, ref[...])
    over_ref[...] = over

    for block in range(BANDS):
        rows = slice(block * HALF, (block + 1) * HALF)
        at = slice((block + 1) * TALL, (block + 2) * TALL)
        for half in range(2):
            lanes = slice(half * 128, (half + 1) * 128)
            total = sums_ref[at, lanes]
            for ref in sums_before:
                total = total + ref[at, lanes]
            feature = feature_of(total)
            wide_ref[rows, lanes] = feature[0:HALF]
            wide_ref[rows, 256 + half * 128 : 256 + (half + 1) * 128] = feature[HALF_PAD : HALF_PAD + HALF]
    feature_ref[...] = wide_ref[...].astype(BF16)


def weights_kernel(weight_ref, w_ref):
    w_ref[...] = jnp.zeros(w_ref.shape, BF16)
    zero = jnp.zeros((PAY - weight_ref.shape[2], 256), F32)
    for shift in range(3):
        for odd in range(2):
            if 2 * shift + odd < 5:
                for tap in range(5):
                    part = weight_ref[tap, 2 * shift + odd].astype(F32)
                    part = jnp.concatenate([part, zero], axis=0).astype(BF16)
                    for out_row in range(2):
                        at = odd * 256 + (tap + 2 * out_row) * PAY
                        w_ref[shift, at : at + PAY, out_row * 256 : (out_row + 1) * 256] = part


def shifted_dots(wide_ref, columns, weights):
    wide_ref[BORDER - 1 : BORDER, :] = wide_ref[BORDER + columns - 1 : BORDER + columns, :]
    wide_ref[BORDER + columns : BORDER + columns + 1, :] = wide_ref[BORDER : BORDER + 1, :]
    total = None
    for shift in range(3):
        start = BORDER + shift - 1
        moved = wide_ref[start : start + columns, :].astype(BF16)
        part = jnp.dot(moved, weights(shift), preferred_element_type=F32)
        total = part if total is None else total + part
    return total


def local_conv_kernel(feature_ref, w_ref, bias_ref, part_ref, wide_ref):
    columns = feature_ref.shape[0]
    shard = lax.axis_index("obs")
    inner = slice(BORDER, BORDER + columns)
    wide_ref[inner, :] = feature_ref[...].astype(F32)
    blank = jnp.zeros((columns, 64), F32)

    @pl.when(shard == 0)
    def _():
        wide_ref[inner, 0:64] = blank
        wide_ref[inner, 256:320] = blank

    @pl.when(shard == lax.axis_size("obs") - 1)
    def _():
        wide_ref[inner, 192:256] = blank
        wide_ref[inner, 448:512] = blank

    bias = jnp.concatenate([bias_ref[...], bias_ref[...]], axis=1)
    part_ref[...] = shifted_dots(wide_ref, columns, lambda shift: w_ref[shift]) + bias


def conv_kernel(part_ref, edge_ref, w_ref, out_ref, wide_ref):
    columns = part_ref.shape[0]
    shard = lax.axis_index("obs")

    def finish(at, out_row):
        wide_ref[BORDER : BORDER + columns, :] = edge_ref[...].astype(F32)
        lanes = slice(out_row * 256, (out_row + 1) * 256)

        def weights(shift):
            rows = [w_ref[shift, odd * 256 + at : odd * 256 + at + 64, lanes] for odd in range(2)]
            return jnp.concatenate(rows, axis=0)

        rest = slice((1 - out_row) * 256, (2 - out_row) * 256)
        out_ref[1 - out_row] = part_ref[:, rest].astype(BF16)
        out_ref[out_row] = (part_ref[:, lanes] + shifted_dots(wide_ref, columns, weights)).astype(BF16)

    first, last = shard == 0, shard == lax.axis_size("obs") - 1

    @pl.when(first)
    def _():
        finish(0, 0)

    @pl.when(last)
    def _():
        finish(192, 1)

    @pl.when(jnp.logical_not(first | last))
    def _():
        out_ref[0] = part_ref[:, 0:256].astype(BF16)
        out_ref[1] = part_ref[:, 256:512].astype(BF16)


def params(mib):
    return pltpu.CompilerParams(vmem_limit_bytes=mib * 2**20)


def vmem():
    return pl.BlockSpec(memory_space=pltpu.VMEM)


def fast_features(values, tile, row, col, frac, place, scale, conv_weight):
    arrivals = tile.shape[0]
    sent = pl.pallas_call(
        pack_kernel,
        out_shape=jax.ShapeDtypeStruct((BANDS * PAY, BOX), BF16),
        in_specs=[vmem()] * 6,
        out_specs=vmem(),
        scratch_shapes=[
            pltpu.VMEM((BANDS * PAY, arrivals), BF16),
            pltpu.VMEM((BOX, arrivals), BF16),
        ],
        compiler_params=params(32),
        name="pack",
    )(
        values,
        tile.reshape(-1, 128),
        row.reshape(-1, 128),
        col.reshape(-1, 128),
        frac,
        place.reshape(2, 128),
    )
    came = lax.all_to_all(sent, "band", split_axis=0, concat_axis=0, tiled=True)
    groups = BANDS + EXTRA
    own = pl.pallas_call(
        regroup_kernel,
        out_shape=jax.ShapeDtypeStruct((groups * PAY, 128), BF16),
        in_specs=[vmem()],
        out_specs=vmem(),
        scratch_shapes=[
            pltpu.VMEM(((groups + 1) // 2 * PAY, BANDS * BOX), BF16),
            pltpu.VMEM((BOX, BANDS * BOX), BF16),
        ],
        compiler_params=params(32),
        name="regroup",
    )(came)
    count = lax.axis_size("obs")
    chips = count // 2

    def along(value, steps):
        order = [(s, ((s // 2 + steps) % chips) * 2 + s % 2) for s in range(count)]
        return lax.ppermute(value, "obs", order)

    def across(value):
        return lax.ppermute(value, "obs", [(s, s ^ 1) for s in range(count)])

    columns = LON // 2
    shape = jax.ShapeDtypeStruct

    def sums(kind, blocks, before=()):
        tall = TALL * (BANDS + 1)
        wide = 128 if kind.startswith("edge") else 256
        slots = SLOTS
        scratch = [
            pltpu.VMEM((slots, wide, len(blocks) * 128), BF16),
            pltpu.VMEM((slots, TALL, len(blocks) * 128), BF16),
            pltpu.VMEM((8, 128), jnp.int32),
            pltpu.SMEM((8, 128), jnp.int32),
            pltpu.SemaphoreType.DMA,
        ]
        over = shape((8, 128), F32)
        if kind == "part":
            out_shape = (shape((tall, wide), F32), over)
        elif kind == "edge_part":
            out_shape = (shape((tall, wide), F32),)
        elif kind == "edge":
            out_shape = (shape((columns, 128), BF16),)
            scratch += [pltpu.VMEM((tall, wide), F32), pltpu.VMEM((columns, 128), F32)]
        else:
            out_shape = (shape((columns, 512), BF16), over)
            scratch += [pltpu.VMEM((tall, wide), F32), pltpu.VMEM((columns, 512), F32)]
        return pl.pallas_call(
            functools.partial(sums_kernel, len(blocks), kind),
            out_shape=out_shape,
            in_specs=[pl.BlockSpec(memory_space=pltpu.SMEM)] + [vmem()] * (len(blocks) + len(before)),
            out_specs=(vmem(),) * len(out_shape),
            scratch_shapes=scratch,
            compiler_params=params(32),
            cost_estimate=pl.CostEstimate(
                flops=len(blocks) * 1_200_000_000, bytes_accessed=len(blocks) * 200_000, transcendentals=0
            ),
            name=kind + "_sums",
        )(scale, *blocks, *before)

    far, after, ahead = (along(own, steps) for steps in (2, 1, -1))
    near = [own, across(own)]
    before = [*sums("part", near), *sums("edge_part", near)]
    conv_weight, *before = lax.optimization_barrier((conv_weight, *before))
    w = pl.pallas_call(
        weights_kernel,
        out_shape=shape((3, 512, 512), BF16),
        in_specs=[vmem()],
        out_specs=vmem(),
        compiler_params=params(32),
        cost_estimate=pl.CostEstimate(flops=1_000_000_000, bytes_accessed=2_000_000, transcendentals=0),
        name="weights",
    )(conv_weight)
    after, ahead, far, w, *before = lax.optimization_barrier((after, ahead, far, w, *before))
    there = [after, ahead, far] + [across(value) for value in (after, ahead, far)]
    *before, edge_before = before
    (edge,) = sums("edge", there, [edge_before])
    edge, *there = lax.optimization_barrier((edge, *there))
    bands = lax.axis_size("band")
    down = [(band * count + SENDS_DOWN, (band + 1) * count) for band in range(bands - 1)]
    up = [(band * count + SENDS_UP, band * count - 1) for band in range(1, bands)]
    edge = lax.ppermute(edge, ("band", "obs"), down + up)
    feature, over = sums("last", there, before)
    return feature, edge, over, w


def from_behind(value, axis, steps):
    count = lax.axis_size(axis)
    first, last = (max(0, -steps), min(count, count - steps))
    return lax.ppermute(value, axis, [(source, source + steps) for source in range(first, last)])


def general(
    obs_values,
    obs_tile,
    obs_row,
    obs_col,
    obs_frac,
    tile_place,
    length_scale,
    conv_weight,
    conv_bias,
):
    band_count = lax.axis_size("band")
    obs_count = lax.axis_size("obs")
    arrivals = obs_tile.shape[0]
    capacity = arrivals // 4
    channels = obs_values.shape[0]
    lat_dev = ROWS_DEV * obs_count
    tile_width = LON // band_count
    band_ids = jnp.arange(band_count, dtype=jnp.int32)
    owner_band = obs_tile % band_count
    within = obs_tile // band_count
    member = (owner_band[:, None] == band_ids[None, :]).astype(jnp.int32)
    slot_rank = jnp.sum(jnp.cumsum(member, axis=0) * member, axis=1) - 1
    target = owner_band * capacity + slot_rank
    payload = jnp.concatenate(
        [
            obs_values.astype(jnp.float32),
            (obs_row.astype(jnp.float32) + obs_frac[0])[None],
            (obs_col.astype(jnp.float32) + obs_frac[1])[None],
            within.astype(jnp.float32)[None],
        ],
        axis=0,
    )
    outbox = (
        jnp.zeros((channels + 3, band_count * capacity), jnp.float32).at[channels + 2].set(-1.0)
    )
    outbox = outbox.at[:, target].set(payload)
    arrived_obs = lax.all_to_all(
        outbox.reshape(channels + 3, band_count, capacity),
        "band",
        split_axis=1,
        concat_axis=1,
        tiled=True,
    )
    inv_lat = 0.5 / (length_scale[0] * length_scale[0])
    inv_lon = 0.5 / (length_scale[1] * length_scale[1])
    row_mid = jnp.arange(lat_dev, dtype=jnp.float32) + 0.5
    col_mid = jnp.arange(tile_width, dtype=jnp.float32) + 0.5
    tile_codes = band_ids.astype(jnp.float32)

    def accumulate(source, running):
        source_block = lax.dynamic_index_in_dim(arrived_obs, source, 1, keepdims=False)
        lat_at = source_block[channels]
        lon_at = source_block[channels + 1]
        slot_at = source_block[channels + 2]
        lat_diff = row_mid[:, None] - lat_at[None, :]
        lon_diff = col_mid[:, None] - lon_at[None, :]
        lat_weight = jnp.exp(-(lat_diff * lat_diff) * inv_lat)
        lon_weight = jnp.exp(-(lon_diff * lon_diff) * inv_lon)
        extended = jnp.concatenate(
            [source_block[:channels], jnp.ones((1, capacity), jnp.float32)], axis=0
        )
        left_factor = (
            (extended[:, None, :] * lat_weight[None])
            .astype(jnp.bfloat16)
            .reshape((channels + 1) * lat_dev, capacity)
        )
        tile_pick = (slot_at[None, :] == tile_codes[:, None]).astype(jnp.float32)
        right_factor = (
            (tile_pick[:, None, :] * lon_weight[None])
            .astype(jnp.bfloat16)
            .reshape(band_count * tile_width, capacity)
        )
        return running + lax.dot_general(
            left_factor, right_factor, (((1,), (1,)), ((), ())), preferred_element_type=jnp.float32
        )

    grid_sums = lax.fori_loop(
        0, band_count, accumulate, jnp.zeros(((channels + 1) * lat_dev, LON), jnp.float32)
    )
    grid_sums = grid_sums.reshape(channels + 1, lat_dev, band_count, tile_width)
    my_band = lax.axis_index("band")
    place_table = tile_place.reshape(band_count, band_count)
    bands_of = place_table // band_count
    blocks_of = place_table % band_count
    my_bands = lax.dynamic_index_in_dim(bands_of, my_band, 1, keepdims=False)
    send_order = jnp.sum(
        (my_bands[None, :] == band_ids[:, None]).astype(jnp.int32) * band_ids[None, :], axis=1
    )
    outgoing = jnp.take(grid_sums, send_order, axis=2)
    matched = (bands_of == my_band).astype(jnp.int32)
    block_of_source = jnp.sum(matched * blocks_of, axis=0)
    source_of_block = jnp.sum(
        (block_of_source[None, :] == band_ids[:, None]).astype(jnp.int32) * band_ids[None, :],
        axis=1,
    )
    arrived = lax.all_to_all(outgoing, "band", split_axis=2, concat_axis=2, tiled=True)
    placed = jnp.take(arrived, source_of_block, axis=2).reshape(channels + 1, lat_dev, LON)
    spread = lax.all_to_all(
        placed.reshape(channels + 1, obs_count, ROWS_DEV, LON), "obs", split_axis=1, concat_axis=1, tiled=True
    )
    band_rows = jnp.sum(spread, axis=1)
    density = band_rows[channels]
    feature = jnp.concatenate(
        [band_rows[:channels] / jnp.maximum(density, 1.0)[None], jnp.log(1.0 + density)[None]],
        axis=0,
    ).astype(jnp.bfloat16)
    rim_lower = from_behind(feature[:, -2:, :], ("band", "obs"), 1)
    rim_upper = from_behind(feature[:, :1, :], ("band", "obs"), -1)
    stacked = jnp.concatenate([rim_lower, feature, rim_upper], axis=1)
    wrapped = jnp.concatenate([stacked[:, :, -2:], stacked, stacked[:, :, :2]], axis=2)
    conv_out = lax.conv_general_dilated(
        wrapped[None],
        conv_weight,
        (2, 2),
        "VALID",
        dimension_numbers=("NCHW", "HWIO", "NHWC"),
        preferred_element_type=jnp.float32,
    )[0]
    return (conv_out + conv_bias).astype(jnp.bfloat16)


def body(*args):
    *_, conv_weight, conv_bias = args
    feature, edge, over, w = fast_features(*args[:8])
    columns = LON // 2
    part = pl.pallas_call(
        local_conv_kernel,
        out_shape=jax.ShapeDtypeStruct((columns, 512), F32),
        in_specs=[vmem()] * 3,
        out_specs=vmem(),
        scratch_shapes=[pltpu.VMEM((columns + 16, 512), F32)],
        compiler_params=params(32),
        cost_estimate=pl.CostEstimate(flops=2_000_000_000, bytes_accessed=4_000_000, transcendentals=0),
        name="local_conv",
    )(feature, w, conv_bias.reshape(1, -1))
    edge, part = lax.optimization_barrier((edge, part))

    def finish(part, edge, w, *args):
        return pl.pallas_call(
            conv_kernel,
            out_shape=jax.ShapeDtypeStruct((2, columns, 256), BF16),
            in_specs=[vmem()] * 3,
            out_specs=vmem(),
            scratch_shapes=[pltpu.VMEM((columns + 16, 128), F32)],
            compiler_params=params(32),
            name="conv",
        )(part, edge, w)

    def whole(part, edge, w, *args):
        return general(*args)

    return lax.cond(over[0, 0] > 0.0, whole, finish, part, edge, w, *args)


def solution(mesh):
    placed = (
        P(None, ("band", "obs")),
        P(("band", "obs")),
        P(("band", "obs")),
        P(("band", "obs")),
        P(None, ("band", "obs")),
        P(),
        P(),
        P(),
        P(),
    )
    return jax.shard_map(
        body, mesh=mesh, in_specs=placed, out_specs=P(("band", "obs"), None, None), check_vma=False
    )
```

```python
import functools

import jax
import jax.numpy as jnp
from jax import lax
from jax.experimental import pallas as pl
from jax.experimental.pallas import tpu as pltpu
from jax.sharding import PartitionSpec as P

LON = 1440
ROWS_DEV = 4
BANDS = 16
TQ = 90
HALF = TQ // 2
HALF_PAD = 48
BOX = 256
EXTRA = 7
HEAD = 4
ROW_CODE = 24
ROW_LAT = 25
ROW_LON = 28
ROW_NOTE = 31
PAY = 32
SLOTS = 8
LAT_BAND = 32
BORDER = 8
SENDS_DOWN = 4
SENDS_UP = 6
ROWS_IN = 7
TALL = 2 * HALF_PAD
LOG2E = 1.4426950408889634
F32 = jnp.float32
BF16 = jnp.bfloat16


def dot_nt(left, right):
    return lax.dot_general(left, right, (((1,), (1,)), ((), ())), preferred_element_type=F32)


def iota(shape, dim):
    return lax.broadcasted_iota(jnp.int32, shape, dim)


def ones_where(mask):
    return jnp.where(mask, 1.0, 0.0)


def ranks(member):
    chunks = len(member)
    rows = chunks * BANDS
    stacked = jnp.concatenate(member, axis=0).astype(BF16)
    before = ones_where(iota((BOX, BOX), 0) < iota((BOX, BOX), 1)).astype(BF16)
    at, of = iota((rows, rows), 0), iota((rows, rows), 1)
    earlier = ones_where(((of & 15) == (at & 15)) & ((of >> 4) < (at >> 4))).astype(BF16)
    inside = jnp.dot(stacked, before, preferred_element_type=F32)
    base = jnp.sum(jnp.dot(earlier, stacked, preferred_element_type=F32), axis=1, keepdims=True)
    place = inside + base
    return [
        jnp.sum(member[k] * place[k * BANDS : (k + 1) * BANDS], axis=0, keepdims=True)
        for k in range(chunks)
    ]


def bucket(payload, group, position, left_ref, right_ref, k):
    lanes = slice(k * BOX, (k + 1) * BOX)
    for g in range(left_ref.shape[0] // PAY):
        left_ref[g * PAY : (g + 1) * PAY, lanes] = jnp.where(group == g, payload, 0.0).astype(BF16)
    right_ref[:, lanes] = ones_where(iota((right_ref.shape[0], BOX), 0) == position).astype(BF16)


def split3(value):
    high = value.astype(BF16).astype(F32)
    rest = value - high
    middle = rest.astype(BF16).astype(F32)
    return high, middle, rest - middle


def pack_kernel(
    values_ref, tile_ref, row_ref, col_ref, frac_ref, place_ref, scale_ref, out_ref, scales_ref, left_ref, right_ref
):
    scale = jnp.where(iota((8, 128), 0) == 0, scale_ref[0], scale_ref[1])
    scales_ref[...] = (-0.5 * LOG2E) / (scale * scale)
    chunks = tile_ref.shape[0] * 128 // BOX

    def wide(ref, k):
        return jnp.concatenate([ref[2 * k : 2 * k + 1, :], ref[2 * k + 1 : 2 * k + 2, :]], axis=1)

    table = jnp.concatenate(
        [jnp.broadcast_to(place_ref[h : h + 1, :].astype(F32), (128, 128)).T for h in range(2)], axis=0
    )
    lines = iota((BOX, 128), 0)
    eight = iota((8, BOX), 0)
    sixteen = iota((BANDS, BOX), 0)
    bands, blocks, member, within = [], [], [], []
    for k in range(chunks):
        place = [
            jnp.sum(jnp.where(lines == tile_ref[at : at + 1, :], table, 0.0), axis=0, keepdims=True)
            for at in (2 * k, 2 * k + 1)
        ]
        place = jnp.concatenate(place, axis=1).astype(jnp.int32)
        bands.append(place >> 4)
        blocks.append(place & 15)
        member.append(ones_where(sixteen == bands[k]))
        within.append(ones_where(sixteen == blocks[k]).astype(BF16))
    counts = dot_nt(jnp.concatenate(member, axis=1).astype(BF16), jnp.concatenate(within, axis=1))
    spread = ones_where((iota((BANDS, BOX), 1) & 15) == sixteen).astype(BF16)
    counts = jnp.dot(counts.astype(BF16), spread, preferred_element_type=F32)
    counts = jnp.sum(jnp.where((iota((BANDS, BOX), 1) >> 4) == sixteen, counts, 0.0), axis=0, keepdims=True)
    rank = ranks(member)
    for k in range(chunks):
        lanes = slice(k * BOX, (k + 1) * BOX)
        lat = split3(wide(row_ref, k).astype(F32) + frac_ref[0:1, lanes])
        lon = split3(wide(col_ref, k).astype(F32) + frac_ref[1:2, lanes])
        tail = jnp.zeros((8, BOX), F32)
        for at, line in enumerate([blocks[k].astype(F32) + 1.0, *lat, *lon]):
            tail = jnp.where(eight == at, line, tail)
        payload = jnp.concatenate([values_ref[:, lanes].astype(F32), tail], axis=0)
        bucket(payload, bands[k], rank[k].astype(jnp.int32), left_ref, right_ref, k)
    packed = dot_nt(left_ref[...], right_ref[...])
    line_of = iota((PAY, BOX), 0)
    for g in range(BANDS):
        rows = slice(g * PAY, (g + 1) * PAY)
        out_ref[rows, :] = jnp.where(line_of == ROW_NOTE, counts, packed[rows]).astype(BF16)


def regroup_kernel(in_ref, out_ref, left_ref, right_ref):
    chunks = in_ref.shape[0] // PAY
    codes, member, notes = [], [], []
    line_of = iota((PAY, BOX), 0)
    total = jnp.zeros((BANDS, 1), F32)
    for k in range(chunks):
        tail = in_ref[k * PAY + 16 : (k + 1) * PAY, :].astype(F32)
        codes.append(tail[ROW_CODE - 16 : ROW_CODE - 15].astype(jnp.int32) - 1)
        notes.append(tail[ROW_NOTE - 16 : ROW_NOTE - 15])
        member.append(ones_where(iota((BANDS, BOX), 0) == codes[k]))
        total = total + jnp.sum(member[k], axis=1, keepdims=True)
    rank = ranks(member)

    more = jnp.maximum(jnp.broadcast_to(total, (BANDS, 128)).astype(jnp.int32) - 1, 0) >> 7
    key = more * BANDS + (BANDS - 1 - iota((BANDS, 128), 0))
    leads = key == jnp.max(key, axis=0, keepdims=True)
    more = jnp.where(leads, jnp.maximum(more, HEAD), more)
    key = more * BANDS + (BANDS - 1 - iota((BANDS, 128), 0))
    more = more.astype(F32)
    first = jnp.zeros((BANDS, 128), F32)
    for g in range(BANDS):
        first = first + jnp.where(key[g : g + 1] > key, more[g : g + 1], 0.0)
    first = jnp.where(leads, 0.0, first)
    last = first + more
    first_wide = jnp.concatenate([first, first], axis=1)

    for k in range(chunks):
        payload = in_ref[k * PAY : (k + 1) * PAY, :].astype(F32)
        payload = jnp.where(line_of == ROW_CODE, 1.0, jnp.where(line_of == ROW_NOTE, 0.0, payload))
        place = rank[k].astype(jnp.int32)
        over = jnp.sum(member[k] * first_wide, axis=0, keepdims=True).astype(jnp.int32)
        group = jnp.where(place < 128, codes[k], BANDS - 1 + over + (place >> 7))
        group = jnp.where(codes[k] < 0, -1, group)
        bucket(payload, group >> 1, (place & 127) + ((group & 1) << 7), left_ref, right_ref, k)
    both = dot_nt(left_ref[...], right_ref[...])

    def moved(group):
        rows = slice((group >> 1) * PAY, (group >> 1) * PAY + PAY)
        return both[rows, 0:128] if group % 2 == 0 else both[rows, 128:256]


    note = jnp.concatenate(notes, axis=0)
    of_band = ones_where((iota((BOX, 128), 0) >> 4) == iota((BOX, 128), 1)).astype(BF16)
    band_sums = jnp.dot(note.astype(BF16), of_band, preferred_element_type=F32)
    tile_sums = jnp.broadcast_to(jnp.sum(note, axis=0, keepdims=True), (BANDS, BOX)).astype(jnp.int32)
    tile_more = jnp.maximum(tile_sums - 1, 0) >> 7
    tile_more = jnp.where((iota((BANDS, BOX), 1) >> 4) == iota((BANDS, BOX), 0), tile_more, 0).astype(F32)
    most = jnp.max(tile_more, axis=1, keepdims=True)
    more_sums = jnp.sum(tile_more, axis=1, keepdims=True) + jnp.maximum(HEAD - most, 0.0)
    band_most = jnp.max(jnp.max(band_sums, axis=1, keepdims=True), axis=0, keepdims=True)
    more_most = jnp.max(more_sums, axis=0, keepdims=True)
    over = jnp.where((band_most > BOX - 1) | (more_most > EXTRA), 1.0, 0.0)

    narrow = iota((PAY, 128), 0)
    out_ref[0:PAY, :] = jnp.where(narrow == ROW_NOTE, over, moved(0)).astype(BF16)
    for g in range(1, BANDS):
        out_ref[g * PAY : (g + 1) * PAY, :] = moved(g).astype(BF16)
    block_code = iota((BANDS, 128), 0).astype(F32) + 1.0
    for e in range(EXTRA):
        rows = slice((BANDS + e) * PAY, (BANDS + e + 1) * PAY)
        code = jnp.where((first <= e) & (last > e), block_code, 0.0)
        code = jnp.sum(code, axis=0, keepdims=True)
        out_ref[rows, :] = jnp.where(narrow == ROW_NOTE, code, moved(BANDS + e)).astype(BF16)


def sums_kernel(count, kind, scale_ref, *refs):
    shard = lax.axis_index("obs")
    if kind.startswith("edge"):

        @pl.when((shard == SENDS_DOWN) | (shard == SENDS_UP))
        def _():
            sums_work(count, kind, shard, scale_ref, *refs)

    else:
        sums_work(count, kind, shard, scale_ref, *refs)


def sums_work(count, kind, shard, scale_ref, *refs):
    last = kind == "last"
    block_refs, refs = refs[:count], refs[count:]
    if last:
        *before_refs, feature_ref, over_ref = refs[:-7]
        left_ref, right_ref, codes_ref, codes_smem, sem, sums_ref, wide_ref = refs[-7:]
    elif kind == "edge":
        before_ref, edge_ref, left_ref, right_ref, codes_ref, codes_smem, sem, sums_ref, wide_ref = refs
    elif kind == "edge_part":
        sums_ref, left_ref, right_ref, codes_ref, codes_smem, sem = refs
    else:
        sums_ref, over_ref, left_ref, right_ref, codes_ref, codes_smem, sem = refs
    wide = sums_ref.shape[1]
    if kind.startswith("edge"):
        rows_in, first_row = 2, jnp.where(shard == SENDS_DOWN, LAT_BAND - 2, 0)
    else:
        rows_in, first_row = ROWS_IN, shard * ROWS_DEV - 2
    lat_scale, lon_scale = scale_ref[0:1, :], scale_ref[1:2, :]
    row_mid = ((iota((8, 128), 0) + first_row) & (LAT_BAND - 1)).astype(F32) + 0.5
    line = iota((2 * HALF_PAD, 128), 0)
    past = (line >= HALF_PAD).astype(jnp.int32)
    col_mid = (2 * (line - HALF_PAD * past) + past).astype(F32) + 0.5
    lane = iota((8, 128), 1)
    sub = iota((8, 128), 0)

    codes = jnp.zeros((8, 128), F32)
    for k in range(count):
        for e in range(EXTRA):
            at = (BANDS + e) * PAY + 16
            note = block_refs[k][at : at + 16, :].astype(F32)[15:16]
            codes = jnp.where((lane == e) & (sub == k), note, codes)
    codes_ref[...] = codes.astype(jnp.int32)
    copy = pltpu.make_async_copy(codes_ref, codes_smem, sem)
    copy.start()

    def factors(start, slot):
        for k in range(count):
            lanes = slice(k * 128, (k + 1) * 128)
            value = block_refs[k][pl.ds(start, PAY), :].astype(F32)
            tail = value[24:32]
            lat_at = tail[1:2] + tail[2:3] + tail[3:4]
            lon_at = tail[4:5] + tail[5:6] + tail[6:7]
            lat_diff = row_mid - lat_at
            lat_weight = jnp.exp2(lat_diff * lat_diff * lat_scale)
            lon_diff = col_mid - lon_at
            lon_weight = jnp.exp2(lon_diff * lon_diff * lon_scale)
            for r in range(rows_in):
                left_ref[slot, r * PAY : (r + 1) * PAY, lanes] = (value * lat_weight[r : r + 1]).astype(BF16)
            right_ref[slot, :, lanes] = lon_weight.astype(BF16)

    slots = left_ref.shape[0]
    for slot in range(slots):
        left_ref[slot, rows_in * PAY :, :] = jnp.zeros((wide - rows_in * PAY, count * 128), BF16)

    def main(p, carry):
        for slot in range(slots):
            at = p * slots + slot
            factors(pl.multiple_of(at * PAY, PAY), slot)
            start = pl.multiple_of((at + 1) * TALL, TALL)
            sums_ref[pl.ds(start, TALL), :] = dot_nt(right_ref[slot], left_ref[slot])
        return carry

    sums_ref[0:TALL, :] = jnp.zeros((TALL, wide), F32)
    lax.fori_loop(0, BANDS // slots, main, 0)

    copy.wait()
    used = jnp.int32(0)
    for e in range(HEAD, EXTRA):
        for k in range(count):
            used = jnp.where(codes_smem[k, e] > 0, e + 1 - HEAD, used)
    for e in range(HEAD):
        factors((BANDS + e) * PAY, e)
    for k in range(count):
        lanes = slice(k * 128, (k + 1) * 128)
        right = jnp.concatenate([right_ref[e, :, lanes] for e in range(HEAD)], axis=1)
        left = jnp.concatenate([left_ref[e, :, lanes] for e in range(HEAD)], axis=1)
        start = pl.multiple_of(codes_smem[k, 0] * TALL, TALL)
        sums_ref[pl.ds(start, TALL), :] += dot_nt(right, left)

    def extra(e, carry):
        factors(pl.multiple_of((BANDS + HEAD + e) * PAY, PAY), 0)
        for k in range(count):
            lanes = slice(k * 128, (k + 1) * 128)
            start = pl.multiple_of(codes_smem[k, HEAD + e] * TALL, TALL)
            sums_ref[pl.ds(start, TALL), :] += dot_nt(right_ref[0, :, lanes], left_ref[0, :, lanes])
        return carry

    lax.fori_loop(0, used, extra, 0)

    channel = iota((TALL, 128), 1) & (PAY - 1)
    dense = iota((TALL, 128), 1) - channel + ROW_CODE

    def feature_of(total):
        density = jnp.take_along_axis(total, dense, axis=1)
        feature = total * (1.0 / jnp.maximum(density, 1.0))
        return jnp.where(channel < 24, feature, jnp.where(channel == 24, jnp.log(1.0 + density), 0.0))

    if kind == "edge_part":
        return
    if kind == "edge":
        for block in range(BANDS):
            rows = slice(block * HALF, (block + 1) * HALF)
            at = slice((block + 1) * TALL, (block + 2) * TALL)
            feature = feature_of(sums_ref[at, :] + before_ref[at, :])
            wide_ref[rows, 0:64] = feature[0:HALF, 0:64]
            wide_ref[rows, 64:128] = feature[HALF_PAD : HALF_PAD + HALF, 0:64]
        edge_ref[...] = wide_ref[...].astype(BF16)
        return

    over = block_refs[0][16:PAY, :].astype(F32)[15:16]
    for k in range(1, count):
        over = jnp.maximum(over, block_refs[k][16:PAY, :].astype(F32)[15:16])
    over = jnp.broadcast_to(over, (8, 128))
    if not last:
        over_ref[...] = over
        return
    sums_before, overs_before = before_refs[0::2], before_refs[1::2]
    for ref in overs_before:
        over = jnp.maximum(over, ref[...])
    over_ref[...] = over

    for block in range(BANDS):
        rows = slice(block * HALF, (block + 1) * HALF)
        at = slice((block + 1) * TALL, (block + 2) * TALL)
        for half in range(2):
            lanes = slice(half * 128, (half + 1) * 128)
            total = sums_ref[at, lanes]
            for ref in sums_before:
                total = total + ref[at, lanes]
            feature = feature_of(total)
            wide_ref[rows, lanes] = feature[0:HALF]
            wide_ref[rows, 256 + half * 128 : 256 + (half + 1) * 128] = feature[HALF_PAD : HALF_PAD + HALF]
    feature_ref[...] = wide_ref[...].astype(BF16)


def weights_kernel(weight_ref, w_ref):
    w_ref[...] = jnp.zeros(w_ref.shape, BF16)
    zero = jnp.zeros((PAY - weight_ref.shape[2], 256), F32)
    for shift in range(3):
        for odd in range(2):
            if 2 * shift + odd < 5:
                for tap in range(5):
                    part = weight_ref[tap, 2 * shift + odd].astype(F32)
                    part = jnp.concatenate([part, zero], axis=0).astype(BF16)
                    for out_row in range(2):
                        at = odd * 256 + (tap + 2 * out_row) * PAY
                        w_ref[shift, at : at + PAY, out_row * 256 : (out_row + 1) * 256] = part


def shifted_dots(wide_ref, columns, weights):
    wide_ref[BORDER - 1 : BORDER, :] = wide_ref[BORDER + columns - 1 : BORDER + columns, :]
    wide_ref[BORDER + columns : BORDER + columns + 1, :] = wide_ref[BORDER : BORDER + 1, :]
    total = None
    for shift in range(3):
        start = BORDER + shift - 1
        moved = wide_ref[start : start + columns, :].astype(BF16)
        part = jnp.dot(moved, weights(shift), preferred_element_type=F32)
        total = part if total is None else total + part
    return total


def local_conv_kernel(feature_ref, w_ref, bias_ref, part_ref, wide_ref):
    columns = feature_ref.shape[0]
    shard = lax.axis_index("obs")
    inner = slice(BORDER, BORDER + columns)
    wide_ref[inner, :] = feature_ref[...].astype(F32)
    blank = jnp.zeros((columns, 64), F32)

    @pl.when(shard == 0)
    def _():
        wide_ref[inner, 0:64] = blank
        wide_ref[inner, 256:320] = blank

    @pl.when(shard == lax.axis_size("obs") - 1)
    def _():
        wide_ref[inner, 192:256] = blank
        wide_ref[inner, 448:512] = blank

    bias = jnp.concatenate([bias_ref[...], bias_ref[...]], axis=1)
    part_ref[...] = shifted_dots(wide_ref, columns, lambda shift: w_ref[shift]) + bias


def conv_kernel(part_ref, edge_ref, w_ref, out_ref, wide_ref):
    columns = part_ref.shape[0]
    shard = lax.axis_index("obs")

    def finish(at, out_row):
        wide_ref[BORDER : BORDER + columns, :] = edge_ref[...].astype(F32)
        lanes = slice(out_row * 256, (out_row + 1) * 256)

        def weights(shift):
            rows = [w_ref[shift, odd * 256 + at : odd * 256 + at + 64, lanes] for odd in range(2)]
            return jnp.concatenate(rows, axis=0)

        rest = slice((1 - out_row) * 256, (2 - out_row) * 256)
        out_ref[1 - out_row] = part_ref[:, rest].astype(BF16)
        out_ref[out_row] = (part_ref[:, lanes] + shifted_dots(wide_ref, columns, weights)).astype(BF16)

    first, last = shard == 0, shard == lax.axis_size("obs") - 1

    @pl.when(first)
    def _():
        finish(0, 0)

    @pl.when(last)
    def _():
        finish(192, 1)

    @pl.when(jnp.logical_not(first | last))
    def _():
        out_ref[0] = part_ref[:, 0:256].astype(BF16)
        out_ref[1] = part_ref[:, 256:512].astype(BF16)


def params(mib):
    return pltpu.CompilerParams(vmem_limit_bytes=mib * 2**20)


def vmem():
    return pl.BlockSpec(memory_space=pltpu.VMEM)


def fast_features(values, tile, row, col, frac, place, scale, conv_weight):
    arrivals = tile.shape[0]
    sent, scales = pl.pallas_call(
        pack_kernel,
        out_shape=(jax.ShapeDtypeStruct((BANDS * PAY, BOX), BF16), jax.ShapeDtypeStruct((8, 128), F32)),
        in_specs=[vmem()] * 6 + [pl.BlockSpec(memory_space=pltpu.SMEM)],
        out_specs=(vmem(), vmem()),
        scratch_shapes=[
            pltpu.VMEM((BANDS * PAY, arrivals), BF16),
            pltpu.VMEM((BOX, arrivals), BF16),
        ],
        compiler_params=params(32),
        name="pack",
    )(
        values,
        tile.reshape(-1, 128),
        row.reshape(-1, 128),
        col.reshape(-1, 128),
        frac,
        place.reshape(2, 128),
        scale,
    )
    came = lax.all_to_all(sent, "band", split_axis=0, concat_axis=0, tiled=True)
    groups = BANDS + EXTRA
    own = pl.pallas_call(
        regroup_kernel,
        out_shape=jax.ShapeDtypeStruct((groups * PAY, 128), BF16),
        in_specs=[vmem()],
        out_specs=vmem(),
        scratch_shapes=[
            pltpu.VMEM(((groups + 1) // 2 * PAY, BANDS * BOX), BF16),
            pltpu.VMEM((BOX, BANDS * BOX), BF16),
        ],
        compiler_params=params(32),
        name="regroup",
    )(came)
    count = lax.axis_size("obs")
    chips = count // 2

    def along(value, steps):
        order = [(s, ((s // 2 + steps) % chips) * 2 + s % 2) for s in range(count)]
        return lax.ppermute(value, "obs", order)

    def across(value):
        return lax.ppermute(value, "obs", [(s, s ^ 1) for s in range(count)])

    columns = LON // 2
    shape = jax.ShapeDtypeStruct

    def sums(kind, blocks, before=()):
        tall = TALL * (BANDS + 1)
        wide = 128 if kind.startswith("edge") else 256
        slots = SLOTS
        scratch = [
            pltpu.VMEM((slots, wide, len(blocks) * 128), BF16),
            pltpu.VMEM((slots, TALL, len(blocks) * 128), BF16),
            pltpu.VMEM((8, 128), jnp.int32),
            pltpu.SMEM((8, 128), jnp.int32),
            pltpu.SemaphoreType.DMA,
        ]
        over = shape((8, 128), F32)
        if kind == "part":
            out_shape = (shape((tall, wide), F32), over)
        elif kind == "edge_part":
            out_shape = (shape((tall, wide), F32),)
        elif kind == "edge":
            out_shape = (shape((columns, 128), BF16),)
            scratch += [pltpu.VMEM((tall, wide), F32), pltpu.VMEM((columns, 128), F32)]
        else:
            out_shape = (shape((columns, 512), BF16), over)
            scratch += [pltpu.VMEM((tall, wide), F32), pltpu.VMEM((columns, 512), F32)]
        return pl.pallas_call(
            functools.partial(sums_kernel, len(blocks), kind),
            out_shape=out_shape,
            in_specs=[vmem()] * (1 + len(blocks) + len(before)),
            out_specs=(vmem(),) * len(out_shape),
            scratch_shapes=scratch,
            compiler_params=params(32),
            cost_estimate=pl.CostEstimate(
                flops=len(blocks) * 1_200_000_000, bytes_accessed=len(blocks) * 200_000, transcendentals=0
            ),
            name=kind + "_sums",
        )(scales, *blocks, *before)

    far, after, ahead = (along(own, steps) for steps in (2, 1, -1))
    near = [own, across(own)]
    before = [*sums("part", near), *sums("edge_part", near)]
    conv_weight, *before = lax.optimization_barrier((conv_weight, *before))
    w = pl.pallas_call(
        weights_kernel,
        out_shape=shape((3, 512, 512), BF16),
        in_specs=[vmem()],
        out_specs=vmem(),
        compiler_params=params(32),
        cost_estimate=pl.CostEstimate(flops=1_000_000_000, bytes_accessed=2_000_000, transcendentals=0),
        name="weights",
    )(conv_weight)
    after, ahead, far, w, *before = lax.optimization_barrier((after, ahead, far, w, *before))
    there = [after, ahead, far] + [across(value) for value in (after, ahead, far)]
    *before, edge_before = before
    (edge,) = sums("edge", there, [edge_before])
    edge, *there = lax.optimization_barrier((edge, *there))
    bands = lax.axis_size("band")
    down = [(band * count + SENDS_DOWN, (band + 1) * count) for band in range(bands - 1)]
    up = [(band * count + SENDS_UP, band * count - 1) for band in range(1, bands)]
    edge = lax.ppermute(edge, ("band", "obs"), down + up)
    feature, over = sums("last", there, before)
    return feature, edge, over, w


def from_behind(value, axis, steps):
    count = lax.axis_size(axis)
    first, last = (max(0, -steps), min(count, count - steps))
    return lax.ppermute(value, axis, [(source, source + steps) for source in range(first, last)])


def general(
    obs_values,
    obs_tile,
    obs_row,
    obs_col,
    obs_frac,
    tile_place,
    length_scale,
    conv_weight,
    conv_bias,
):
    band_count = lax.axis_size("band")
    obs_count = lax.axis_size("obs")
    arrivals = obs_tile.shape[0]
    capacity = arrivals // 4
    channels = obs_values.shape[0]
    lat_dev = ROWS_DEV * obs_count
    tile_width = LON // band_count
    band_ids = jnp.arange(band_count, dtype=jnp.int32)
    owner_band = obs_tile % band_count
    within = obs_tile // band_count
    member = (owner_band[:, None] == band_ids[None, :]).astype(jnp.int32)
    slot_rank = jnp.sum(jnp.cumsum(member, axis=0) * member, axis=1) - 1
    target = owner_band * capacity + slot_rank
    payload = jnp.concatenate(
        [
            obs_values.astype(jnp.float32),
            (obs_row.astype(jnp.float32) + obs_frac[0])[None],
            (obs_col.astype(jnp.float32) + obs_frac[1])[None],
            within.astype(jnp.float32)[None],
        ],
        axis=0,
    )
    outbox = (
        jnp.zeros((channels + 3, band_count * capacity), jnp.float32).at[channels + 2].set(-1.0)
    )
    outbox = outbox.at[:, target].set(payload)
    arrived_obs = lax.all_to_all(
        outbox.reshape(channels + 3, band_count, capacity),
        "band",
        split_axis=1,
        concat_axis=1,
        tiled=True,
    )
    inv_lat = 0.5 / (length_scale[0] * length_scale[0])
    inv_lon = 0.5 / (length_scale[1] * length_scale[1])
    row_mid = jnp.arange(lat_dev, dtype=jnp.float32) + 0.5
    col_mid = jnp.arange(tile_width, dtype=jnp.float32) + 0.5
    tile_codes = band_ids.astype(jnp.float32)

    def accumulate(source, running):
        source_block = lax.dynamic_index_in_dim(arrived_obs, source, 1, keepdims=False)
        lat_at = source_block[channels]
        lon_at = source_block[channels + 1]
        slot_at = source_block[channels + 2]
        lat_diff = row_mid[:, None] - lat_at[None, :]
        lon_diff = col_mid[:, None] - lon_at[None, :]
        lat_weight = jnp.exp(-(lat_diff * lat_diff) * inv_lat)
        lon_weight = jnp.exp(-(lon_diff * lon_diff) * inv_lon)
        extended = jnp.concatenate(
            [source_block[:channels], jnp.ones((1, capacity), jnp.float32)], axis=0
        )
        left_factor = (
            (extended[:, None, :] * lat_weight[None])
            .astype(jnp.bfloat16)
            .reshape((channels + 1) * lat_dev, capacity)
        )
        tile_pick = (slot_at[None, :] == tile_codes[:, None]).astype(jnp.float32)
        right_factor = (
            (tile_pick[:, None, :] * lon_weight[None])
            .astype(jnp.bfloat16)
            .reshape(band_count * tile_width, capacity)
        )
        return running + lax.dot_general(
            left_factor, right_factor, (((1,), (1,)), ((), ())), preferred_element_type=jnp.float32
        )

    grid_sums = lax.fori_loop(
        0, band_count, accumulate, jnp.zeros(((channels + 1) * lat_dev, LON), jnp.float32)
    )
    grid_sums = grid_sums.reshape(channels + 1, lat_dev, band_count, tile_width)
    my_band = lax.axis_index("band")
    place_table = tile_place.reshape(band_count, band_count)
    bands_of = place_table // band_count
    blocks_of = place_table % band_count
    my_bands = lax.dynamic_index_in_dim(bands_of, my_band, 1, keepdims=False)
    send_order = jnp.sum(
        (my_bands[None, :] == band_ids[:, None]).astype(jnp.int32) * band_ids[None, :], axis=1
    )
    outgoing = jnp.take(grid_sums, send_order, axis=2)
    matched = (bands_of == my_band).astype(jnp.int32)
    block_of_source = jnp.sum(matched * blocks_of, axis=0)
    source_of_block = jnp.sum(
        (block_of_source[None, :] == band_ids[:, None]).astype(jnp.int32) * band_ids[None, :],
        axis=1,
    )
    arrived = lax.all_to_all(outgoing, "band", split_axis=2, concat_axis=2, tiled=True)
    placed = jnp.take(arrived, source_of_block, axis=2).reshape(channels + 1, lat_dev, LON)
    spread = lax.all_to_all(
        placed.reshape(channels + 1, obs_count, ROWS_DEV, LON), "obs", split_axis=1, concat_axis=1, tiled=True
    )
    band_rows = jnp.sum(spread, axis=1)
    density = band_rows[channels]
    feature = jnp.concatenate(
        [band_rows[:channels] / jnp.maximum(density, 1.0)[None], jnp.log(1.0 + density)[None]],
        axis=0,
    ).astype(jnp.bfloat16)
    rim_lower = from_behind(feature[:, -2:, :], ("band", "obs"), 1)
    rim_upper = from_behind(feature[:, :1, :], ("band", "obs"), -1)
    stacked = jnp.concatenate([rim_lower, feature, rim_upper], axis=1)
    wrapped = jnp.concatenate([stacked[:, :, -2:], stacked, stacked[:, :, :2]], axis=2)
    conv_out = lax.conv_general_dilated(
        wrapped[None],
        conv_weight,
        (2, 2),
        "VALID",
        dimension_numbers=("NCHW", "HWIO", "NHWC"),
        preferred_element_type=jnp.float32,
    )[0]
    return (conv_out + conv_bias).astype(jnp.bfloat16)


def body(*args):
    *_, conv_weight, conv_bias = args
    feature, edge, over, w = fast_features(*args[:8])
    columns = LON // 2
    part = pl.pallas_call(
        local_conv_kernel,
        out_shape=jax.ShapeDtypeStruct((columns, 512), F32),
        in_specs=[vmem()] * 3,
        out_specs=vmem(),
        scratch_shapes=[pltpu.VMEM((columns + 16, 512), F32)],
        compiler_params=params(32),
        cost_estimate=pl.CostEstimate(flops=2_000_000_000, bytes_accessed=4_000_000, transcendentals=0),
        name="local_conv",
    )(feature, w, conv_bias.reshape(1, -1))
    edge, part = lax.optimization_barrier((edge, part))

    def finish(part, edge, w, *args):
        return pl.pallas_call(
            conv_kernel,
            out_shape=jax.ShapeDtypeStruct((2, columns, 256), BF16),
            in_specs=[vmem()] * 3,
            out_specs=vmem(),
            scratch_shapes=[pltpu.VMEM((columns + 16, 128), F32)],
            compiler_params=params(32),
            name="conv",
        )(part, edge, w)

    def whole(part, edge, w, *args):
        return general(*args)

    return lax.cond(over[0, 0] > 0.0, whole, finish, part, edge, w, *args)


def solution(mesh):
    placed = (
        P(None, ("band", "obs")),
        P(("band", "obs")),
        P(("band", "obs")),
        P(("band", "obs")),
        P(None, ("band", "obs")),
        P(),
        P(),
        P(),
        P(),
    )
    return jax.shard_map(
        body, mesh=mesh, in_specs=placed, out_specs=P(("band", "obs"), None, None), check_vma=False
    )
```
